32 devices in a mesh: fold: 2 (over y), vox: 16 (over z, x, core).
Axes of the slice: x: 2, y: 2, z: 4, core: 2. Of those that a mesh axis runs over, the one named last changes fastest.
Arguments:
- volumes: float32 [1024, 12288], P('fold', 'vox'), parts along dimension 0, may hold values from -6 to 6
- record_index: int32 [512], P('fold'), parts along dimension 0, may hold values from 0 to 511
- fold_of: int32 [1024], P('fold'), parts along dimension 0, may hold values from 0 to 4
- held_out: int32 [2], P('fold'), parts along dimension 0, may hold values from 0 to 4
- dictionary: float32 [12288, 512], P('vox'), may hold values from -1 to 1
Outputs:
- new_dictionary: float32 [24576, 512], P(('fold', 'vox')), parts along dimension 0
- code_matrix: float32 [512, 512], P('fold'), parts along dimension 0
- dict_gram: float32 [1024, 512], P('fold'), parts along dimension 0
The draws below stay inside these ranges and needn't reach their ends.
There are 2 independent parts, one for each index of `fold`. The reference program is written for one: setup_inputs(seed, part) draws one part's arguments, and reference() takes and returns one part's arrays. A program takes and returns all parts, laid end to end along the dimension named above; an argument that names none is the same for every part. Nothing has to cross between parts.
All inputs are finite; a program needn't handle non-finite values.
Results may differ from the reference program's by a relative error of at most 0.0001.
Values sent between devices are 32-bit elements; how exact they have to be, the bound alone decides.
No kernel may reach another device: no remote copies, remote signals or barrier semaphores. Data moves between devices by JAX's collectives and lax.ppermute only.
A program may use at most 64 MiB of HBM per device.

```python
import math
import jax
import jax.numpy as jnp
from jax import lax

ATOMS = 512
BATCH = 256
RECORDS = 512
FOLDS = 5
ISTA_STEPS = 5
DICT_STEPS = 2
VOXELS = 12288


def draw_dictionary(key, part):
    entry_key = jax.random.fold_in(key, 11)
    pick_key = jax.random.fold_in(key, 12)
    factor_key = jax.random.fold_in(key, 13)
    base = jnp.clip(jax.random.normal(entry_key, (VOXELS, ATOMS), jnp.float32), -6.0, 6.0)
    placing = jax.random.permutation(pick_key, ATOMS)
    weak_atom = placing < ATOMS // 8
    shrunk = jax.random.uniform(factor_key, (ATOMS,), jnp.float32, 0.15, 0.25)
    column_factor = jnp.where(weak_atom, shrunk, jnp.float32(1.0))
    return (base * column_factor[None, :] / math.sqrt(VOXELS)).astype(jnp.float32)


def touch_ends(result, rng, least, largest):
    spot = [jax.random.randint(jax.random.fold_in(rng, axis), (), 0, length) for axis, length in enumerate(result.shape)]
    widest = result.shape.index(max(result.shape))
    next_to = spot[:widest] + [(spot[widest] + 1) % result.shape[widest]] + spot[widest + 1:]
    return result.at[tuple(spot)].set(least).at[tuple(next_to)].set(largest)


def levels(rng, shape, split, low, high):
    factor_of = 1.0
    for dim, blocks in split:
        steps = jax.random.uniform(jax.random.fold_in(jax.random.fold_in(rng, 6), dim), (blocks,), jnp.float32, low / len(split), high / len(split))
        factor_of = factor_of * jnp.repeat(jnp.exp(steps), shape[dim] // blocks).reshape((-1,) + (1,) * (len(shape) - 1 - dim))
    return factor_of


def gaussian(rng, shape, spread, most, cuts=(), dtype=jnp.bfloat16):
    drawn = jax.random.normal(rng, shape, jnp.float32) * spread
    if len(cuts) > 0:
        drawn = levels(rng, shape, cuts, -0.22, 0.18) * drawn
    return jnp.clip(drawn, min=-most, max=most).astype(dtype)


def setup_inputs(seed: int = 0, part: int = 0) -> dict:
    key_of = jax.random.split(jax.random.key(seed), 6)
    part_keys = jax.random.split(jax.random.fold_in(key_of[5], part), 6)
    return {
        "volumes": gaussian(part_keys[0], (RECORDS, VOXELS), 1.0, 6.0, ((1, 16),), jnp.float32),
        "record_index": touch_ends(jax.random.randint(part_keys[1], (BATCH,), 0, RECORDS), jax.random.fold_in(part_keys[1], 1), 0, RECORDS - 1).astype(jnp.int32),
        "fold_of": touch_ends(jax.random.randint(part_keys[2], (RECORDS,), 0, FOLDS), jax.random.fold_in(part_keys[2], 1), 0, FOLDS - 1).astype(jnp.int32),
        "held_out": jax.random.randint(part_keys[3], (1,), 0, FOLDS).astype(jnp.int32),
        "dictionary": draw_dictionary(jax.random.fold_in(key_of[5], 71), part),
    }


penalty = 0.5

def matmul(left, right):
    return jnp.dot(left, right, precision=lax.Precision.HIGHEST, preferred_element_type=jnp.float32)

def row_bound(matrix):
    return jnp.max(lax.optimization_barrier(jnp.sum(jnp.abs(matrix), axis=1)))

def reference(volumes, record_index, fold_of, held_out, dictionary):
    batch_rows = volumes[record_index]
    weight = (fold_of[record_index] != held_out[0]).astype(jnp.float32)
    correlation = matmul(batch_rows, dictionary)
    gram_total = matmul(dictionary.T, dictionary)
    bound = row_bound(gram_total)
    code_rows = jnp.zeros_like(correlation)
    for sweep in range(ISTA_STEPS):
        moved = code_rows - (matmul(code_rows, gram_total) - correlation) / bound
        limit = penalty / bound
        code_rows = moved - jnp.clip(moved, -limit, limit)
    weighted = code_rows * weight[:, None]
    moment = matmul(code_rows.T, weighted)
    target = matmul(batch_rows.T, weighted)
    step_size = 1.0 / (1.0 + row_bound(moment))
    current = dictionary
    for sweep in range(DICT_STEPS):
        stepped = current - step_size * (matmul(current, moment) - target)
        lengths = jnp.sqrt(lax.optimization_barrier(jnp.sum(stepped * stepped, axis=0)))
        current = stepped / jnp.maximum(lengths, 1.0)
    dict_gram = matmul(current.T, current)
    return (current, code_rows, dict_gram)
```

```python
import functools

import jax
import jax.numpy as jnp
from jax import lax
from jax.experimental import pallas as pl
from jax.experimental.pallas import tpu as pltpu
from jax.sharding import PartitionSpec as P

ISTA_STEPS = 5
PENALTY = 0.5
TILE = 128
F32 = jnp.float32
BF16 = jnp.bfloat16

NN = (((1,), (0,)), ((), ()))
TN = (((0,), (0,)), ((), ()))
NT = (((1,), (1,)), ((), ()))


def halves(x):
    hi = x.astype(BF16)
    return hi, (x - hi.astype(F32)).astype(BF16)


def dot1(a, b, dims=NN):
    return lax.dot_general(a, b, dims, preferred_element_type=F32)


def dot3(a, b, dims=NN):
    return dot1(a[0], b[0], dims) + (dot1(a[0], b[1], dims) + dot1(a[1], b[0], dims))


def top_row_sum(x):
    return jnp.max(jnp.sum(jnp.abs(x), axis=1, keepdims=True), axis=0, keepdims=True)


def upper_tiles(batch, atoms):
    edge = (batch + atoms) // TILE
    return [(r, c) for r in range(edge) for c in range(r, edge)]


def slot_of(vox, bits):
    place = 0
    for k in range(bits):
        place = place + ((vox >> k) & 1) * (1 << (bits - 1 - k))
    return place


def gram_kernel(tiles, bits, index_ref, fold_ref, held_ref, volumes_ref, dict_ref,
                keep_ref, send_ref, bhi_ref, blo_ref, weight_ref, full):
    batch = index_ref.shape[1]
    records = volumes_ref.shape[0]
    atoms = dict_ref.shape[1]
    d = halves(dict_ref[...])
    for r in range(0, atoms, 256):
        left = (d[0][:, r:r + 256], d[1][:, r:r + 256])
        right = (d[0][:, r:], d[1][:, r:])
        full[batch + r:batch + r + 256, batch + r:] = dot3(left, right, TN)
    pick = lax.broadcasted_iota(jnp.int32, (records, batch), 0) == index_ref[...]
    pick = pick.astype(F32).astype(BF16)
    v = halves(volumes_ref[...])
    b = (dot1(pick, v[0], TN).astype(BF16), dot1(pick, v[1], TN).astype(BF16))
    bhi_ref[...] = b[0]
    blo_ref[...] = b[1]
    full[:batch, batch:] = dot3(b, d)
    full[:batch, :batch] = dot3(b, b, NT)
    fold = jnp.broadcast_to(fold_ref[...], (TILE, records)).astype(F32).astype(BF16)
    folds = dot1(pick, fold, (((0,), (1,)), ((), ())))
    weight_ref[...] = jnp.where(folds != held_ref[0].astype(F32), 1.0, 0.0)
    slots = 1 << bits
    rows = TILE // slots
    mine = slot_of(lax.axis_index("vox"), bits)
    half = slots // 2
    for o in range(slots):
        out = keep_ref if o < half else send_ref
        start = (mine ^ o) * rows
        for k, (r, c) in enumerate(tiles):
            at = pl.multiple_of(r * TILE + start, rows)
            out[o % half, k * rows:(k + 1) * rows, :] = full[pl.ds(at, rows), c * TILE:(c + 1) * TILE]


def step_kernel(tiles, bits, mine_ref, other_ref, bhi_ref, blo_ref, weight_ref, dict_ref,
                new_ref, code_ref, gram_ref, full):
    batch = bhi_ref.shape[0]
    atoms = dict_ref.shape[1]
    slots = 1 << bits
    rows = TILE // slots
    half = slots // 2
    place = slot_of(lax.axis_index("vox"), bits)
    for o in range(slots):
        source = mine_ref if o < half else other_ref
        start = (place ^ o) * rows
        for k, (r, c) in enumerate(tiles):
            at = pl.multiple_of(r * TILE + start, rows)
            full[pl.ds(at, rows), c * TILE:(c + 1) * TILE] = source[o % half, k * rows:(k + 1) * rows, :]
    for r, c in tiles:
        if r != c and (r * TILE >= batch or c * TILE < batch):
            full[c * TILE:(c + 1) * TILE, r * TILE:(r + 1) * TILE] = full[r * TILE:(r + 1) * TILE, c * TILE:(c + 1) * TILE].T
    gram = full[batch:, batch:]
    bound = top_row_sum(gram)
    inverse = 1.0 / bound
    limit = PENALTY * inverse
    g = halves(gram)
    corr = full[:batch, batch:]
    moved = corr * inverse
    code = moved - jnp.clip(moved, -limit, limit)
    for _ in range(ISTA_STEPS - 1):
        moved = code - (dot3(halves(code), g) - corr) * inverse
        code = moved - jnp.clip(moved, -limit, limit)
    code_ref[...] = code
    weight = jnp.concatenate([weight_ref[...]] * (atoms // TILE), axis=1)
    weighted = code * weight
    w = halves(weighted)
    moment = dot3(w, w, TN)
    step = 1.0 / (1.0 + top_row_sum(moment))
    diagonal = lax.broadcasted_iota(jnp.int32, (atoms, atoms), 0) == lax.broadcasted_iota(jnp.int32, (atoms, atoms), 1)
    eye = jnp.where(diagonal, 1.0, 0.0)
    pull = eye - step * moment
    p = halves(pull)
    c = halves(corr)
    k = halves(full[:batch, :batch])
    kw = step * dot3(k, w)
    cw = step * dot3(c, w, TN)
    upper = dot3(c, p) + kw
    lower = dot3(g, p) + cw
    squares = jnp.sum(pull * lower, axis=0, keepdims=True) + step * jnp.sum(weighted * upper, axis=0, keepdims=True)
    scale = 1.0 / jnp.sqrt(jnp.maximum(squares, 1.0))
    top = halves(step * (dot3(halves(weighted * scale), p) + weighted))
    bottom = halves(dot3(halves(pull * scale), p))
    upper = dot3(halves(upper * scale), p) + kw
    lower = dot3(halves(lower * scale), p) + cw
    raw = dot3(top, halves(upper), TN) + dot3(bottom, halves(lower), TN)
    lengths = jnp.sum(raw * eye, axis=0, keepdims=True)
    lengths_down = jnp.sum(raw * eye, axis=1, keepdims=True)
    scale = 1.0 / jnp.sqrt(jnp.maximum(lengths, 1.0))
    scale_down = 1.0 / jnp.sqrt(jnp.maximum(lengths_down, 1.0))
    gram_ref[...] = raw * scale * scale_down
    b = (bhi_ref[...], blo_ref[...])
    d = halves(dict_ref[...])
    new_ref[...] = (dot3(b, top, TN) + dot3(d, bottom)) * scale


def all_reduce(keep, send, devices, bits):
    def swap(x, bit):
        return lax.ppermute(x, "vox", [(i, i ^ bit) for i in range(devices)])

    total = keep + swap(send, 1)
    mid = bits - 1
    flips = []
    for o in range(1 << mid):
        flips.append(sum(1 << (bits - 1 - j) for j in range(mid) if (o >> j) & 1))
    parts = [total[o] for o in range(1 << mid)]
    got = [swap(parts[o], flips[o]) for o in range(1, 1 << mid)]
    own = parts[0]
    for part in got:
        own = own + part
    for bit in range(bits, devices.bit_length() - 1):
        own = own + swap(own, 1 << bit)
    mine = jnp.stack([own] + [swap(own, flips[o]) for o in range(1, 1 << mid)])
    return mine, swap(mine, 1)


def shards(devices, volumes, record_index, fold_of, held_out, dictionary):
    records, voxels = volumes.shape
    batch = record_index.shape[0]
    atoms = dictionary.shape[1]
    tiles = upper_tiles(batch, atoms)
    bits = 3
    slots = 1 << bits
    part = jax.ShapeDtypeStruct((slots // 2, len(tiles) * TILE // slots, TILE), F32)
    vmem = pl.BlockSpec(memory_space=pltpu.VMEM)
    smem = pl.BlockSpec(memory_space=pltpu.SMEM)
    full = pltpu.VMEM((batch + atoms, batch + atoms), F32)
    params = pltpu.CompilerParams(vmem_limit_bytes=48 << 20)
    keep, send, bhi, blo, weight = pl.pallas_call(
        functools.partial(gram_kernel, tiles, bits),
        out_shape=(part, part, jax.ShapeDtypeStruct((batch, voxels), BF16),
                   jax.ShapeDtypeStruct((batch, voxels), BF16), jax.ShapeDtypeStruct((batch, TILE), F32)),
        in_specs=[vmem, vmem, smem, vmem, vmem],
        out_specs=(vmem,) * 5,
        scratch_shapes=[full],
        compiler_params=params,
        name="grams",
    )(record_index[None], fold_of[None], held_out, volumes, dictionary)
    mine, other = all_reduce(keep, send, devices, bits)
    return pl.pallas_call(
        functools.partial(step_kernel, tiles, bits),
        out_shape=(jax.ShapeDtypeStruct(dictionary.shape, F32), jax.ShapeDtypeStruct((batch, atoms), F32),
                   jax.ShapeDtypeStruct((atoms, atoms), F32)),
        in_specs=[vmem] * 6,
        out_specs=(vmem,) * 3,
        scratch_shapes=[full],
        compiler_params=params,
        name="step",
    )(mine, other, bhi, blo, weight, dictionary)


def solution(mesh):
    devices = mesh.shape["vox"]
    in_specs = (P("fold", "vox"), P("fold"), P("fold"), P("fold"), P("vox", None))
    out_specs = (P(("fold", "vox"), None), P("fold", None), P("fold", None))
    return jax.shard_map(functools.partial(shards, devices), mesh=mesh, in_specs=in_specs, out_specs=out_specs, check_vma=False)
```

```python
import functools

import jax
import jax.numpy as jnp
from jax import lax
from jax.experimental import pallas as pl
from jax.experimental.pallas import tpu as pltpu
from jax.sharding import PartitionSpec as P

ISTA_STEPS = 5
PENALTY = 0.5
TILE = 128
F32 = jnp.float32
BF16 = jnp.bfloat16

NN = (((1,), (0,)), ((), ()))
TN = (((0,), (0,)), ((), ()))
NT = (((1,), (1,)), ((), ()))


def halves(x):
    hi = x.astype(BF16)
    return hi, (x - hi.astype(F32)).astype(BF16)


def dot1(a, b, dims=NN):
    return lax.dot_general(a, b, dims, preferred_element_type=F32)


def dot3(a, b, dims=NN):
    return dot1(a[0], b[0], dims) + (dot1(a[0], b[1], dims) + dot1(a[1], b[0], dims))


def top_row_sum(x):
    return jnp.max(jnp.sum(jnp.abs(x), axis=1, keepdims=True), axis=0, keepdims=True)


def upper_tiles(batch, atoms):
    edge = (batch + atoms) // TILE
    return [(r, c) for r in range(edge) for c in range(r, edge)]


def slot_of(vox, bits):
    place = 0
    for k in range(bits):
        bit = (vox >> k) & 1
        if k == bits - 1:
            bit = bit ^ ((vox >> bits) & 1)
        place = place + bit * (1 << (bits - 1 - k))
    return place


def column(row):
    return jnp.broadcast_to(row, (TILE, row.shape[1])).T[:, :1]


def gram_kernel(tiles, bits, index_hbm, fold_hbm, held_ref, volumes_hbm, dict_hbm,
                keep_ref, send_ref, flipped_ref, weight_ref, index_ref, fold_ref, volumes_ref, dict_ref, full, sems):
    pairs = ((dict_hbm, dict_ref), (index_hbm, index_ref), (fold_hbm, fold_ref), (volumes_hbm, volumes_ref))
    copies = [pltpu.make_async_copy(source, target, sems.at[j]) for j, (source, target) in enumerate(pairs)]
    for copy in copies:
        copy.start()
    batch = index_ref.shape[1]
    records = volumes_ref.shape[0]
    atoms = dict_ref.shape[1]
    copies[0].wait()
    d = halves(dict_ref[...])
    for r in range(0, atoms, 256):
        left = (d[0][:, r:r + 256], d[1][:, r:r + 256])
        right = (d[0][:, r:], d[1][:, r:])
        full[batch + r:batch + r + 256, batch + r:] = dot3(left, right, TN)
    for copy in copies[1:]:
        copy.wait()
    pick = lax.broadcasted_iota(jnp.int32, (records, batch), 0) == index_ref[...]
    pick = pick.astype(F32).astype(BF16)
    v = halves(volumes_ref[...])
    b = (dot1(pick, v[0], TN), dot1(pick, v[1], TN))
    flipped_ref[...] = (b[0] + b[1]).T
    b = (b[0].astype(BF16), b[1].astype(BF16))
    full[:batch, batch:] = dot3(b, d)
    full[:batch, :batch] = dot3(b, b, NT)
    fold = jnp.broadcast_to(fold_ref[...], (TILE, records)).astype(F32).astype(BF16)
    folds = dot1(pick, fold, (((0,), (1,)), ((), ())))
    weight_ref[...] = jnp.where(folds != held_ref[0].astype(F32), 1.0, 0.0)
    slots = 1 << bits
    rows = TILE // slots
    mine = slot_of(lax.axis_index("vox"), bits)
    half = slots // 2
    for o in range(slots):
        out = keep_ref if o < half else send_ref
        start = (mine ^ o) * rows
        for k, (r, c) in enumerate(tiles):
            at = pl.multiple_of(r * TILE + start, rows)
            out[o % half, k * rows:(k + 1) * rows, :] = full[pl.ds(at, rows), c * TILE:(c + 1) * TILE]


def step_kernel(tiles, bits, mine_ref, other_ref, flipped_ref, weight_ref, dict_ref,
                new_hbm, code_hbm, gram_hbm, full, new_ref, code_ref, gram_ref, sems):
    batch = flipped_ref.shape[1]
    voxels, atoms = dict_ref.shape
    slots = 1 << bits
    rows = TILE // slots
    half = slots // 2
    place = slot_of(lax.axis_index("vox"), bits)
    for o in range(slots):
        source = mine_ref if o < half else other_ref
        start = (place ^ o) * rows
        for k, (r, c) in enumerate(tiles):
            at = pl.multiple_of(r * TILE + start, rows)
            full[pl.ds(at, rows), c * TILE:(c + 1) * TILE] = source[o % half, k * rows:(k + 1) * rows, :]
    for r, c in tiles:
        if r != c and (r * TILE >= batch or c * TILE < batch):
            full[c * TILE:(c + 1) * TILE, r * TILE:(r + 1) * TILE] = full[r * TILE:(r + 1) * TILE, c * TILE:(c + 1) * TILE].T

    gram = full[batch:, batch:]
    bound = top_row_sum(gram)
    inverse = 1.0 / bound
    limit = PENALTY * inverse
    g = halves(gram)
    corr = full[:batch, batch:]
    moved = corr * inverse
    code = moved - jnp.clip(moved, -limit, limit)
    groups = [slice(0, batch // 2), slice(batch // 2, batch)]
    codes = [code[group] for group in groups]
    for _ in range(ISTA_STEPS - 1):
        for j, group in enumerate(groups):
            moved = codes[j] - (dot3(halves(codes[j]), g) - corr[group]) * inverse
            codes[j] = moved - jnp.clip(moved, -limit, limit)
    code = jnp.concatenate(codes, axis=0)
    code_ref[...] = code
    code_copy = pltpu.make_async_copy(code_ref, code_hbm, sems.at[0])
    code_copy.start()

    x = halves(code)
    weighted = code * jnp.concatenate([weight_ref[...]] * (atoms // TILE), axis=1)
    w = halves(weighted)
    step = 1.0 / (1.0 + top_row_sum(dot3(w, w, TN)))

    block = voxels // 3 if voxels % 3 == 0 and (voxels // 3) % 16 == 0 else voxels
    rows_of = [slice(at, at + block) for at in range(0, voxels, block)]

    def pulled(now, here):
        return dot3(halves(flipped_ref[here, :] - dot3(halves(now), x, NT)), w)

    for here in rows_of:
        new_ref[here, :] = pulled(dict_ref[here, :], here)

    def half_change(gram_now, corr_now):
        fit = corr_now - dot3(x, halves(gram_now))
        cross = full[:batch, :batch] - dot3(halves(corr_now), x, NT)
        square = cross - dot3(x, halves(fit), NT)
        return cross, fit + (0.5 * step) * dot3(halves(square), w)

    tile_eye = lax.broadcasted_iota(jnp.int32, (TILE, TILE), 0) == lax.broadcasted_iota(jnp.int32, (TILE, TILE), 1)
    squares = jnp.concatenate(
        [jnp.sum(jnp.where(tile_eye, gram[r:r + TILE, r:r + TILE], 0.0), axis=0, keepdims=True)
         for r in range(0, atoms, TILE)], axis=1)
    cross, change = half_change(gram, corr)
    squares = squares + 2.0 * step * jnp.sum(weighted * change, axis=0, keepdims=True)
    scale = 1.0 / jnp.sqrt(jnp.maximum(squares, 1.0))
    outer = dot3(w, halves(change), TN)
    gram = (gram + step * (outer + outer.T)) * scale * column(scale)
    corr = (corr + step * dot3(halves(cross), w)) * scale
    squares = squares * scale * scale
    _, change = half_change(gram, corr)
    squares = squares + 2.0 * step * jnp.sum(weighted * change, axis=0, keepdims=True)
    last_scale = 1.0 / jnp.sqrt(jnp.maximum(squares, 1.0))
    outer = dot3(w, halves(change), TN)
    gram_ref[...] = (gram + step * (outer + outer.T)) * last_scale * column(last_scale)
    gram_copy = pltpu.make_async_copy(gram_ref, gram_hbm, sems.at[1])
    gram_copy.start()

    copies = [code_copy, gram_copy]
    for j, here in enumerate(rows_of):
        now = (dict_ref[here, :] + step * new_ref[here, :]) * scale
        new_ref[here, :] = (now + step * pulled(now, here)) * last_scale
        copy = pltpu.make_async_copy(new_ref.at[here, :], new_hbm.at[here, :], sems.at[2 + j])
        copy.start()
        copies.append(copy)
    for copy in copies:
        copy.wait()


def all_reduce(keep, send, devices, bits):
    def swap(x, bit):
        return lax.ppermute(x, "vox", [(i, i ^ bit) for i in range(devices)])

    total = keep + swap(send, 1)
    mid = bits - 1
    flips = []
    for o in range(1 << mid):
        flips.append(sum(1 << (bits - 1 - j) for j in range(mid) if (o >> j) & 1))
    parts = [total[o] for o in range(1 << mid)]
    got = [swap(parts[o], flips[o]) for o in range(1, 1 << mid)]
    own = parts[0]
    for part in got:
        own = own + part
    for k in range(bits, devices.bit_length() - 1):
        own = own + swap(own, 3 << (k - 1) if k == bits else 1 << k)
    mine = jnp.stack([own] + [swap(own, flips[o]) for o in range(1, 1 << mid)])
    return mine, swap(mine, 1)


def pin(x):
    return pltpu.with_memory_space_constraint(x, pltpu.HBM)


def shards(devices, volumes, record_index, fold_of, held_out, dictionary):
    records, voxels = volumes.shape
    batch = record_index.shape[0]
    atoms = dictionary.shape[1]
    tiles = upper_tiles(batch, atoms)
    bits = 3
    slots = 1 << bits
    part = jax.ShapeDtypeStruct((slots // 2, len(tiles) * TILE // slots, TILE), F32)
    vmem = pl.BlockSpec(memory_space=pltpu.VMEM)
    smem = pl.BlockSpec(memory_space=pltpu.SMEM)
    hbm = pl.BlockSpec(memory_space=pltpu.HBM)
    full = pltpu.VMEM((batch + atoms, batch + atoms), F32)
    params = pltpu.CompilerParams(vmem_limit_bytes=48 << 20)
    keep, send, flipped, weight = pl.pallas_call(
        functools.partial(gram_kernel, tiles, bits),
        out_shape=(part, part, jax.ShapeDtypeStruct((voxels, batch), F32), jax.ShapeDtypeStruct((batch, TILE), F32)),
        in_specs=[hbm, hbm, smem, hbm, hbm],
        out_specs=(vmem,) * 4,
        scratch_shapes=[pltpu.VMEM((1, batch), jnp.int32), pltpu.VMEM((1, records), jnp.int32),
                        pltpu.VMEM(volumes.shape, F32), pltpu.VMEM(dictionary.shape, F32), full,
                        pltpu.SemaphoreType.DMA((4,))],
        compiler_params=params,
        name="grams",
    )(pin(record_index[None]), pin(fold_of[None]), held_out, pin(volumes), pin(dictionary))
    mine, other = all_reduce(keep, send, devices, bits)
    outs = [dictionary.shape, (batch, atoms), (atoms, atoms)]
    return pl.pallas_call(
        functools.partial(step_kernel, tiles, bits),
        out_shape=tuple(jax.ShapeDtypeStruct(shape, F32) for shape in outs),
        in_specs=[vmem] * 5,
        out_specs=(hbm,) * 3,
        scratch_shapes=[full] + [pltpu.VMEM(shape, F32) for shape in outs] + [pltpu.SemaphoreType.DMA((5,))],
        compiler_params=params,
        name="step",
    )(mine, other, flipped, weight, dictionary)


def solution(mesh):
    devices = mesh.shape["vox"]
    in_specs = (P("fold", "vox"), P("fold"), P("fold"), P("fold"), P("vox", None))
    out_specs = (P(("fold", "vox"), None), P("fold", None), P("fold", None))
    return jax.shard_map(functools.partial(shards, devices), mesh=mesh, in_specs=in_specs, out_specs=out_specs, check_vma=False)
```

```python
import functools

import jax
import jax.numpy as jnp
from jax import lax
from jax.experimental import pallas as pl
from jax.experimental.pallas import tpu as pltpu
from jax.sharding import PartitionSpec as P

ISTA_STEPS = 5
PENALTY = 0.5
TILE = 128
SPARE = 8
BITS = 3
SQUARE = (4, 6, 2)
F32 = jnp.float32
BF16 = jnp.bfloat16

NN = (((1,), (0,)), ((), ()))
TN = (((0,), (0,)), ((), ()))
NT = (((1,), (1,)), ((), ()))


def halves(x):
    hi = x.astype(BF16)
    return hi, (x - hi.astype(F32)).astype(BF16)


def dot1(a, b, dims=NN):
    return lax.dot_general(a, b, dims, preferred_element_type=F32)


def dot3(a, b, dims=NN):
    return dot1(a[0], b[0], dims) + (dot1(a[0], b[1], dims) + dot1(a[1], b[0], dims))


def top_row_sum(x):
    return jnp.max(jnp.sum(jnp.abs(x), axis=1, keepdims=True), axis=0, keepdims=True)


def upper_tiles(first, count):
    ends = range(first, first + count)
    return [(r, c) for r in ends for c in ends if c > r], [(r, r + 1) for r in ends[::2]]


def layout(batch, atoms):
    edge, wide = batch // TILE, atoms // TILE
    grams = []
    for fold in range(2):
        plain, pairs = upper_tiles(edge + fold * wide // 2, wide // 2)
        strip = range(edge + fold * wide // 4, edge + (fold + 1) * wide // 4)
        plain = plain + [(r, c) for r in strip for c in range(edge + wide // 2, edge + wide)]
        grams.append((pairs, plain))
    plain, pairs = upper_tiles(0, edge)
    rest = (pairs, plain + [(r, c) for r in range(edge) for c in range(edge, edge + wide)])
    return grams, rest


def slot_of(vox):
    x = (vox >> 1) & 1
    z = ((vox >> 2) ^ (vox >> 3)) & 1
    return (vox & 1) * 4 + x * 2 + (x ^ z)


def column(row):
    return jnp.broadcast_to(row, (TILE, row.shape[1])).T[:, :1]


def eye_tile():
    rows = lax.broadcasted_iota(jnp.int32, (TILE, TILE), 0)
    columns = lax.broadcasted_iota(jnp.int32, (TILE, TILE), 1)
    return rows, columns


def pack(pairs, plain, block, first, stage, at):
    rows, columns = eye_tile()

    def tile(r, c):
        r, c = (r - first[0]) * TILE, (c - first[1]) * TILE
        return block[r:r + TILE, c:c + TILE]

    apart = []
    for one, other in pairs:
        low = tile(other, other)
        stage[at * TILE:(at + 1) * TILE, :] = jnp.where(rows <= columns, tile(one, one), low)
        apart.append(jnp.sum(jnp.where(rows == columns, low, 0.0), axis=0, keepdims=True))
        at += 1
    for r, c in plain:
        stage[at * TILE:(at + 1) * TILE, :] = tile(r, c)
        at += 1
    return apart, at


def gram_kernel(index_hbm, fold_hbm, held_ref, volumes_hbm, dict_hbm,
                keep_ref, send_ref, flipped_ref, weight_ref, index_ref, fold_ref, volumes_ref, dict_ref, stage, sems):
    pairs = ((dict_hbm, dict_ref), (index_hbm, index_ref), (fold_hbm, fold_ref), (volumes_hbm, volumes_ref))
    copies = [pltpu.make_async_copy(source, target, sems.at[j]) for j, (source, target) in enumerate(pairs)]
    for copy in copies:
        copy.start()
    batch = index_ref.shape[1]
    records = volumes_ref.shape[0]
    atoms = dict_ref.shape[1]
    edge = batch // TILE
    wide = atoms // TILE
    grams, (rest_pairs, rest_plain) = layout(batch, atoms)
    fold = lax.axis_index("fold") & 1
    copies[0].wait()
    d = halves(dict_ref[...])
    far = slice(atoms // 2, atoms)
    mine = halves(dict_ref[:, pl.ds(pl.multiple_of(fold * (atoms // 2), TILE), atoms // 2)])
    strip = halves(dict_ref[:, pl.ds(pl.multiple_of(fold * (atoms // 4), TILE), atoms // 4)])
    near, plain = grams[0]
    apart, at = pack(near, [t for t in plain if t[1] < edge + wide // 2], dot3(mine, mine, TN), (edge, edge), stage, 0)
    _, at = pack([], [t for t in plain if t[1] >= edge + wide // 2],
                 dot3(strip, (d[0][:, far], d[1][:, far]), TN), (edge, edge + wide // 2), stage, at)
    first = at
    for copy in copies[1:]:
        copy.wait()
    pick = lax.broadcasted_iota(jnp.int32, (records, batch), 0) == index_ref[...]
    pick = pick.astype(F32).astype(BF16)
    v = halves(volumes_ref[...])
    b = (dot1(pick, v[0], TN), dot1(pick, v[1], TN))
    flipped_ref[...] = (b[0] + b[1]).T
    b = (b[0].astype(BF16), b[1].astype(BF16))
    own, at = pack(rest_pairs, [t for t in rest_plain if t[1] < edge], dot3(b, b, NT), (0, 0), stage, at)
    _, at = pack([], [t for t in rest_plain if t[1] >= edge], dot3(b, d), (0, edge), stage, at)
    folds = jnp.broadcast_to(fold_ref[...], (TILE, records)).astype(F32).astype(BF16)
    folds = dot1(pick, folds, (((0,), (1,)), ((), ())))
    weight_ref[...] = jnp.where(folds != held_ref[0].astype(F32), 1.0, 0.0)

    place = lax.broadcasted_iota(jnp.int32, (SPARE, TILE), 0) - fold * (SPARE // 2)
    spare = jnp.zeros((SPARE, TILE), F32)
    for j, row in enumerate(apart + own):
        spare = spare + jnp.where(place == j, row, 0.0)
    slots = 1 << BITS
    rows = TILE // slots
    me = slot_of(lax.axis_index("vox"))
    half = slots // 2
    for o in range(slots):
        out = keep_ref if o < half else send_ref
        which = me ^ o
        base = o % half * (at * rows + SPARE)
        for k in range(at):
            to = base + k * rows + (SPARE if k >= first else 0)
            out[to:to + rows, :] = stage[pl.ds(pl.multiple_of(k * TILE + which * rows, rows), rows), :]
        out[base + first * rows:base + first * rows + SPARE, :] = jnp.where(which == 0, spare, 0.0)


def step_kernel(mine_ref, other_ref, flipped_ref, weight_ref, dict_ref,
                new_hbm, code_hbm, gram_hbm, full, stage, new_ref, code_ref, gram_ref, sems):
    batch = flipped_ref.shape[1]
    voxels, atoms = dict_ref.shape
    slots = 1 << BITS
    rows = TILE // slots
    half = slots // 2
    place = slot_of(lax.axis_index("vox"))
    grams, rest = layout(batch, atoms)
    kinds = []
    for pairs, plain in grams + [rest]:
        kinds += [(pair, True) for pair in pairs] + [(tile, False) for tile in plain]
    split = len(kinds) - len(rest[0]) - len(rest[1])
    spare = jnp.zeros((SPARE, TILE), F32)
    for o in range(slots):
        source = mine_ref if o < half else other_ref
        start = (place ^ o) * rows
        base = o % half * (len(kinds) * rows + SPARE)
        packed = 0
        for k, ((r, c), pair) in enumerate(kinds):
            at = base + k * rows + (SPARE if k >= split else 0)
            value = source[at:at + rows, :]
            if pair:
                stage[pl.ds(pl.multiple_of(packed * TILE + start, rows), rows), :] = value
                packed += 1
            else:
                full[pl.ds(pl.multiple_of(r * TILE + start, rows), rows), c * TILE:(c + 1) * TILE] = value
        spare = spare + source[base + split * rows:base + split * rows + SPARE, :]
    across, down = eye_tile()
    own = len(grams[0][0])
    mate = lax.axis_index("fold") & 1
    packed = 0
    for k, ((r, c), pair) in enumerate(kinds):
        if pair:
            value = stage[packed * TILE:(packed + 1) * TILE, :]
            turned = value.T
            if packed < 2 * own:
                at = packed // own * (SPARE // 2) + packed % own
                diagonal = spare[at:at + 1, :]
            else:
                at = own + packed - 2 * own
                diagonal = jnp.where(mate == 0, spare[at:at + 1, :], spare[at + SPARE // 2:at + SPARE // 2 + 1, :])
            packed += 1
            full[r * TILE:(r + 1) * TILE, r * TILE:(r + 1) * TILE] = jnp.where(across <= down, value, turned)
            full[c * TILE:(c + 1) * TILE, c * TILE:(c + 1) * TILE] = jnp.where(
                across == down, diagonal, jnp.where(across > down, value, turned))
        elif r * TILE >= batch or c * TILE < batch:
            full[c * TILE:(c + 1) * TILE, r * TILE:(r + 1) * TILE] = full[r * TILE:(r + 1) * TILE, c * TILE:(c + 1) * TILE].T

    gram = full[batch:, batch:]
    bound = top_row_sum(gram)
    inverse = 1.0 / bound
    limit = PENALTY * inverse
    g = halves(gram)
    corr = full[:batch, batch:]
    moved = corr * inverse
    code = moved - jnp.clip(moved, -limit, limit)
    groups = [slice(0, batch // 2), slice(batch // 2, batch)]
    codes = [code[group] for group in groups]
    for _ in range(ISTA_STEPS - 1):
        for j, group in enumerate(groups):
            moved = codes[j] - (dot3(halves(codes[j]), g) - corr[group]) * inverse
            codes[j] = moved - jnp.clip(moved, -limit, limit)
    code = jnp.concatenate(codes, axis=0)
    code_ref[...] = code
    code_copy = pltpu.make_async_copy(code_ref, code_hbm, sems.at[0])
    code_copy.start()

    x = halves(code)
    weighted = code * jnp.concatenate([weight_ref[...]] * (atoms // TILE), axis=1)
    w = halves(weighted)
    step = 1.0 / (1.0 + top_row_sum(dot3(w, w, TN)))

    block = voxels // 3 if voxels % 3 == 0 and (voxels // 3) % 16 == 0 else voxels
    rows_of = [slice(at, at + block) for at in range(0, voxels, block)]

    def pulled(now, here):
        return dot3(halves(flipped_ref[here, :] - dot3(halves(now), x, NT)), w)

    for here in rows_of:
        new_ref[here, :] = pulled(dict_ref[here, :], here)

    def half_change(gram_now, corr_now):
        fit = corr_now - dot3(x, halves(gram_now))
        cross = full[:batch, :batch] - dot3(halves(corr_now), x, NT)
        square = cross - dot3(x, halves(fit), NT)
        return cross, fit + (0.5 * step) * dot3(halves(square), w)

    tile_eye = lax.broadcasted_iota(jnp.int32, (TILE, TILE), 0) == lax.broadcasted_iota(jnp.int32, (TILE, TILE), 1)
    squares = jnp.concatenate(
        [jnp.sum(jnp.where(tile_eye, gram[r:r + TILE, r:r + TILE], 0.0), axis=0, keepdims=True)
         for r in range(0, atoms, TILE)], axis=1)
    cross, change = half_change(gram, corr)
    squares = squares + 2.0 * step * jnp.sum(weighted * change, axis=0, keepdims=True)
    scale = 1.0 / jnp.sqrt(jnp.maximum(squares, 1.0))
    outer = dot3(w, halves(change), TN)
    gram = (gram + step * (outer + outer.T)) * scale * column(scale)
    corr = (corr + step * dot3(halves(cross), w)) * scale
    squares = squares * scale * scale
    _, change = half_change(gram, corr)
    squares = squares + 2.0 * step * jnp.sum(weighted * change, axis=0, keepdims=True)
    last_scale = 1.0 / jnp.sqrt(jnp.maximum(squares, 1.0))
    outer = dot3(w, halves(change), TN)
    gram_ref[...] = (gram + step * (outer + outer.T)) * last_scale * column(last_scale)
    gram_copy = pltpu.make_async_copy(gram_ref, gram_hbm, sems.at[1])
    gram_copy.start()

    copies = [code_copy, gram_copy]
    for j, here in enumerate(rows_of):
        now = (dict_ref[here, :] + step * new_ref[here, :]) * scale
        new_ref[here, :] = (now + step * pulled(now, here)) * last_scale
        copy = pltpu.make_async_copy(new_ref.at[here, :], new_hbm.at[here, :], sems.at[2 + j])
        copy.start()
        copies.append(copy)
    for copy in copies:
        copy.wait()


def all_reduce(keep, send, gram_rows, devices, folds):
    def swap(x, bit):
        return lax.ppermute(x, "vox", [(i, i ^ bit) for i in range(devices)])

    total = keep + swap(send, 1)
    slot = total.shape[0] // (len(SQUARE) + 1)
    own = total[:slot]
    got = [swap(total[(k + 1) * slot:(k + 2) * slot], bit) for k, bit in enumerate(SQUARE)]
    for part in got:
        own = own + part
    gram, rest = own[:gram_rows + SPARE], own[gram_rows + SPARE:]
    gram, rest = lax.optimization_barrier((gram, rest))
    for k in range(BITS, devices.bit_length() - 1):
        bit = 3 << (k - 1) if k == BITS else 1 << k
        other = swap(rest, bit), swap(gram, bit)
        gram, rest = gram + other[1], rest + other[0]
    next_gram = lax.ppermute(gram, "fold", [(i, i ^ 1) for i in range(folds)])
    next_gram, rest = lax.optimization_barrier((next_gram, rest))
    even = lax.axis_index("fold") & 1 == 0
    first = jnp.where(even, gram[:gram_rows], next_gram[:gram_rows])
    second = jnp.where(even, next_gram[:gram_rows], gram[:gram_rows])
    own = jnp.concatenate([first, second, gram[gram_rows:] + next_gram[gram_rows:], rest])
    mine = jnp.concatenate([own] + [swap(own, bit) for bit in SQUARE])
    return mine, swap(mine, 1)


def pin(x):
    return pltpu.with_memory_space_constraint(x, pltpu.HBM)


def shards(devices, folds, volumes, record_index, fold_of, held_out, dictionary):
    records, voxels = volumes.shape
    batch = record_index.shape[0]
    atoms = dictionary.shape[1]
    grams, rest = layout(batch, atoms)
    gram_tiles, rest_tiles = (len(pairs) + len(plain) for pairs, plain in (grams[0], rest))
    slots = 1 << BITS
    part = jax.ShapeDtypeStruct((slots // 2 * ((gram_tiles + rest_tiles) * TILE // slots + SPARE), TILE), F32)
    vmem = pl.BlockSpec(memory_space=pltpu.VMEM)
    smem = pl.BlockSpec(memory_space=pltpu.SMEM)
    hbm = pl.BlockSpec(memory_space=pltpu.HBM)
    params = pltpu.CompilerParams(vmem_limit_bytes=48 << 20)
    keep, send, flipped, weight = pl.pallas_call(
        gram_kernel,
        out_shape=(part, part, jax.ShapeDtypeStruct((voxels, batch), F32), jax.ShapeDtypeStruct((batch, TILE), F32)),
        in_specs=[hbm, hbm, smem, hbm, hbm],
        out_specs=(vmem,) * 4,
        scratch_shapes=[pltpu.VMEM((1, batch), jnp.int32), pltpu.VMEM((1, records), jnp.int32),
                        pltpu.VMEM(volumes.shape, F32), pltpu.VMEM(dictionary.shape, F32),
                        pltpu.VMEM(((gram_tiles + rest_tiles) * TILE, TILE), F32),
                        pltpu.SemaphoreType.DMA((4,))],
        compiler_params=params,
        name="grams",
    )(pin(record_index[None]), pin(fold_of[None]), held_out, pin(volumes), pin(dictionary))
    mine, other = all_reduce(keep, send, gram_tiles * TILE // slots, devices, folds)
    outs = [dictionary.shape, (batch, atoms), (atoms, atoms)]
    return pl.pallas_call(
        step_kernel,
        out_shape=tuple(jax.ShapeDtypeStruct(shape, F32) for shape in outs),
        in_specs=[vmem] * 5,
        out_specs=(hbm,) * 3,
        scratch_shapes=[pltpu.VMEM((batch + atoms, batch + atoms), F32), pltpu.VMEM(((batch + atoms) // 2, TILE), F32)]
        + [pltpu.VMEM(shape, F32) for shape in outs] + [pltpu.SemaphoreType.DMA((5,))],
        compiler_params=params,
        name="step",
    )(mine, other, flipped, weight, dictionary)


def solution(mesh):
    in_specs = (P("fold", "vox"), P("fold"), P("fold"), P("fold"), P("vox", None))
    out_specs = (P(("fold", "vox"), None), P("fold", None), P("fold", None))
    return jax.shard_map(functools.partial(shards, mesh.shape["vox"], mesh.shape["fold"]), mesh=mesh, in_specs=in_specs, out_specs=out_specs, check_vma=False)
```

```python
import functools

import jax
import jax.numpy as jnp
from jax import lax
from jax.experimental import pallas as pl
from jax.experimental.pallas import tpu as pltpu
from jax.sharding import PartitionSpec as P

ISTA_STEPS = 5
PENALTY = 0.5
TILE = 128
SPARE = 8
BITS = 3
SQUARE = (4, 6, 2)
F32 = jnp.float32
BF16 = jnp.bfloat16

NN = (((1,), (0,)), ((), ()))
TN = (((0,), (0,)), ((), ()))
NT = (((1,), (1,)), ((), ()))


def halves(x):
    hi = x.astype(BF16)
    return hi, (x - hi.astype(F32)).astype(BF16)


def dot1(a, b, dims=NN):
    return lax.dot_general(a, b, dims, preferred_element_type=F32)


def dot3(a, b, dims=NN):
    (left,), _ = dims[0]
    rows = a[0].shape[1 - left]
    both = dot1(jnp.concatenate(a, axis=1 - left), b[0], dims)
    return both[:rows] + (both[rows:] + dot1(a[0], b[1], dims))


def square3(a, b, dims=NN):
    mixed = dot1(a[0], b[1], dims)
    return dot1(a[0], b[0], dims) + (mixed + mixed.T)


def top_row_sum(x):
    return jnp.max(jnp.sum(jnp.abs(x), axis=1, keepdims=True), axis=0, keepdims=True)


def upper_tiles(first, count):
    ends = range(first, first + count)
    return [(r, c) for r in ends for c in ends if c > r], [(r, r + 1) for r in ends[::2]]


def layout(batch, atoms):
    edge, wide = batch // TILE, atoms // TILE
    grams = []
    for fold in range(2):
        plain, pairs = upper_tiles(edge + fold * wide // 2, wide // 2)
        strip = range(edge + fold * wide // 4, edge + (fold + 1) * wide // 4)
        plain = plain + [(r, c) for r in strip for c in range(edge + wide // 2, edge + wide)]
        grams.append((pairs, plain))
    plain, pairs = upper_tiles(0, edge)
    rest = (pairs, plain + [(r, c) for r in range(edge) for c in range(edge, edge + wide)])
    return grams, rest


def slot_of(vox):
    x = (vox >> 1) & 1
    z = ((vox >> 2) ^ (vox >> 3)) & 1
    return (vox & 1) * 4 + x * 2 + (x ^ z)


def column(row):
    return jnp.broadcast_to(row, (TILE, row.shape[1])).T[:, :1]


def eye_tile():
    rows = lax.broadcasted_iota(jnp.int32, (TILE, TILE), 0)
    columns = lax.broadcasted_iota(jnp.int32, (TILE, TILE), 1)
    return rows, columns


def pack(pairs, plain, block, first, stage, at):
    rows, columns = eye_tile()

    def tile(r, c):
        r, c = (r - first[0]) * TILE, (c - first[1]) * TILE
        return block[r:r + TILE, c:c + TILE]

    apart = []
    for one, other in pairs:
        low = tile(other, other)
        stage[at * TILE:(at + 1) * TILE, :] = jnp.where(rows <= columns, tile(one, one), low)
        apart.append(jnp.sum(jnp.where(rows == columns, low, 0.0), axis=0, keepdims=True))
        at += 1
    for r, c in plain:
        stage[at * TILE:(at + 1) * TILE, :] = tile(r, c)
        at += 1
    return apart, at


def gram_kernel(index_hbm, fold_hbm, held_ref, volumes_hbm, dict_hbm,
                keep_ref, send_ref, flipped_ref, weight_ref, index_ref, fold_ref, volumes_ref, dict_ref, stage, sems):
    pairs = ((index_hbm, index_ref), (fold_hbm, fold_ref), (volumes_hbm, volumes_ref), (dict_hbm, dict_ref))
    copies = [pltpu.make_async_copy(source, target, sems.at[j]) for j, (source, target) in enumerate(pairs)]
    for copy in copies:
        copy.start()
    batch = index_ref.shape[1]
    records = volumes_ref.shape[0]
    atoms = dict_ref.shape[1]
    edge = batch // TILE
    wide = atoms // TILE
    grams, (rest_pairs, rest_plain) = layout(batch, atoms)
    fold = lax.axis_index("fold") & 1
    for copy in copies[:-1]:
        copy.wait()
    pick = lax.broadcasted_iota(jnp.int32, (records, batch), 0) == index_ref[...]
    pick = pick.astype(F32).astype(BF16)
    v = halves(volumes_ref[...])
    b = (dot1(pick, v[0], TN), dot1(pick, v[1], TN))
    flipped_ref[...] = (b[0] + b[1]).T
    b = (b[0].astype(BF16), b[1].astype(BF16))
    copies[-1].wait()
    d = halves(dict_ref[...])
    far = slice(atoms // 2, atoms)
    mine = halves(dict_ref[:, pl.ds(pl.multiple_of(fold * (atoms // 2), TILE), atoms // 2)])
    strip = halves(dict_ref[:, pl.ds(pl.multiple_of(fold * (atoms // 4), TILE), atoms // 4)])
    near, plain = grams[0]
    apart, at = pack(near, [t for t in plain if t[1] < edge + wide // 2], square3(mine, mine, TN), (edge, edge), stage, 0)
    _, at = pack([], [t for t in plain if t[1] >= edge + wide // 2],
                 dot3(strip, (d[0][:, far], d[1][:, far]), TN), (edge, edge + wide // 2), stage, at)
    first = at
    own, at = pack(rest_pairs, [t for t in rest_plain if t[1] < edge], square3(b, b, NT), (0, 0), stage, at)
    _, at = pack([], [t for t in rest_plain if t[1] >= edge], dot3(b, d), (0, edge), stage, at)
    folds = jnp.broadcast_to(fold_ref[...], (TILE, records)).astype(F32).astype(BF16)
    folds = dot1(pick, folds, (((0,), (1,)), ((), ())))
    weight_ref[...] = jnp.where(folds != held_ref[0].astype(F32), 1.0, 0.0)

    place = lax.broadcasted_iota(jnp.int32, (SPARE, TILE), 0) - fold * (SPARE // 2)
    spare = jnp.zeros((SPARE, TILE), F32)
    for j, row in enumerate(apart + own):
        spare = spare + jnp.where(place == j, row, 0.0)
    slots = 1 << BITS
    rows = TILE // slots
    me = slot_of(lax.axis_index("vox"))
    half = slots // 2
    for o in range(slots):
        out = keep_ref if o < half else send_ref
        which = me ^ o
        base = o % half * (at * rows + SPARE)
        for k in range(at):
            to = base + k * rows + (SPARE if k >= first else 0)
            out[to:to + rows, :] = stage[pl.ds(pl.multiple_of(k * TILE + which * rows, rows), rows), :]
        out[base + first * rows:base + first * rows + SPARE, :] = jnp.where(which == 0, spare, 0.0)


def step_kernel(mine_ref, other_ref, flipped_ref, weight_ref, dict_ref,
                new_hbm, code_hbm, gram_hbm, full, stage, new_ref, code_ref, gram_ref, sems):
    batch = flipped_ref.shape[1]
    voxels, atoms = dict_ref.shape
    slots = 1 << BITS
    rows = TILE // slots
    half = slots // 2
    place = slot_of(lax.axis_index("vox"))
    grams, rest = layout(batch, atoms)
    kinds = []
    for pairs, plain in grams + [rest]:
        kinds += [(pair, True) for pair in pairs] + [(tile, False) for tile in plain]
    split = len(kinds) - len(rest[0]) - len(rest[1])
    spare = jnp.zeros((SPARE, TILE), F32)
    for o in range(slots):
        source = mine_ref if o < half else other_ref
        start = (place ^ o) * rows
        base = o % half * (len(kinds) * rows + SPARE)
        packed = 0
        for k, ((r, c), pair) in enumerate(kinds):
            at = base + k * rows + (SPARE if k >= split else 0)
            value = source[at:at + rows, :]
            if pair:
                stage[pl.ds(pl.multiple_of(packed * TILE + start, rows), rows), :] = value
                packed += 1
            else:
                full[pl.ds(pl.multiple_of(r * TILE + start, rows), rows), c * TILE:(c + 1) * TILE] = value
        spare = spare + source[base + split * rows:base + split * rows + SPARE, :]
    across, down = eye_tile()
    own = len(grams[0][0])
    mate = lax.axis_index("fold") & 1
    packed = 0
    for k, ((r, c), pair) in enumerate(kinds):
        if pair:
            value = stage[packed * TILE:(packed + 1) * TILE, :]
            turned = value.T
            if packed < 2 * own:
                at = packed // own * (SPARE // 2) + packed % own
                diagonal = spare[at:at + 1, :]
            else:
                at = own + packed - 2 * own
                diagonal = jnp.where(mate == 0, spare[at:at + 1, :], spare[at + SPARE // 2:at + SPARE // 2 + 1, :])
            packed += 1
            full[r * TILE:(r + 1) * TILE, r * TILE:(r + 1) * TILE] = jnp.where(across <= down, value, turned)
            full[c * TILE:(c + 1) * TILE, c * TILE:(c + 1) * TILE] = jnp.where(
                across == down, diagonal, jnp.where(across > down, value, turned))
        elif r * TILE >= batch or c * TILE < batch:
            full[c * TILE:(c + 1) * TILE, r * TILE:(r + 1) * TILE] = full[r * TILE:(r + 1) * TILE, c * TILE:(c + 1) * TILE].T

    gram = full[batch:, batch:]
    bound = top_row_sum(gram)
    inverse = 1.0 / bound
    limit = PENALTY * inverse
    g = halves(gram)
    corr = full[:batch, batch:]
    moved = corr * inverse
    code = moved - jnp.clip(moved, -limit, limit)
    groups = [slice(0, batch // 2), slice(batch // 2, batch)]
    codes = [code[group] for group in groups]
    for _ in range(ISTA_STEPS - 1):
        for j, group in enumerate(groups):
            moved = codes[j] - (dot3(halves(codes[j]), g) - corr[group]) * inverse
            codes[j] = moved - jnp.clip(moved, -limit, limit)
    code = jnp.concatenate(codes, axis=0)
    code_ref[...] = code
    code_copy = pltpu.make_async_copy(code_ref, code_hbm, sems.at[0])
    code_copy.start()

    x = halves(code)
    weighted = code * jnp.concatenate([weight_ref[...]] * (atoms // TILE), axis=1)
    w = halves(weighted)
    turned_w = halves(weighted.T)
    fit = corr - dot3(x, g)

    def residuals(corr_now, now):
        both = dot3(halves(jnp.concatenate([corr_now, now], axis=0)), x, NT)
        return full[:batch, :batch] - both[:batch], flipped_ref[...] - both[batch:]

    cross, rest = residuals(corr, dict_ref[...])
    step = 1.0 / (1.0 + top_row_sum(square3(turned_w, w)))
    square = cross - dot3(x, halves(fit), NT)
    tile_eye = across == down
    squares = jnp.concatenate(
        [jnp.sum(jnp.where(tile_eye, gram[r:r + TILE, r:r + TILE], 0.0), axis=0, keepdims=True)
         for r in range(0, atoms, TILE)], axis=1)
    moves = dot3(halves(jnp.concatenate([square, cross, rest], axis=0)), w)
    change = fit + (0.5 * step) * moves[:batch]
    squares = squares + 2.0 * step * jnp.sum(weighted * change, axis=0, keepdims=True)
    scale = 1.0 / jnp.sqrt(jnp.maximum(squares, 1.0))
    outer = dot3(turned_w, halves(change))
    corr = (corr + step * moves[batch:2 * batch]) * scale
    now = (dict_ref[...] + step * moves[2 * batch:]) * scale
    new_ref[...] = now
    cross, rest = residuals(corr, now)
    gram = (gram + step * (outer + outer.T)) * scale * column(scale)
    fit = corr - dot3(x, halves(gram))
    square = cross - dot3(x, halves(fit), NT)
    squares = squares * scale * scale
    moves = dot3(halves(jnp.concatenate([square, rest], axis=0)), w)
    change = fit + (0.5 * step) * moves[:batch]
    squares = squares + 2.0 * step * jnp.sum(weighted * change, axis=0, keepdims=True)
    scale = 1.0 / jnp.sqrt(jnp.maximum(squares, 1.0))
    copies = [code_copy]
    block = voxels // 3 if voxels % 3 == 0 and (voxels // 3) % 16 == 0 else voxels
    for j in range(voxels // block):
        here = slice(j * block, (j + 1) * block)
        new_ref[here, :] = (new_ref[here, :] + step * moves[batch + j * block:batch + (j + 1) * block]) * scale
        copies.append(pltpu.make_async_copy(new_ref.at[here, :], new_hbm.at[here, :], sems.at[2 + j]))
        copies[-1].start()
    outer = dot3(turned_w, halves(change))
    gram_ref[...] = (gram + step * (outer + outer.T)) * scale * column(scale)
    copies.append(pltpu.make_async_copy(gram_ref, gram_hbm, sems.at[1]))
    copies[-1].start()
    for copy in copies:
        copy.wait()


def all_reduce(keep, send, gram_rows, devices, folds):
    def swap(x, bit):
        return lax.ppermute(x, "vox", [(i, i ^ bit) for i in range(devices)])

    total = keep + swap(send, 1)
    slot = total.shape[0] // (len(SQUARE) + 1)
    own = total[:slot]
    got = [swap(total[(k + 1) * slot:(k + 2) * slot], bit) for k, bit in enumerate(SQUARE)]
    for part in got:
        own = own + part
    gram, rest = own[:gram_rows + SPARE], own[gram_rows + SPARE:]
    gram, rest = lax.optimization_barrier((gram, rest))
    for k in range(BITS, devices.bit_length() - 1):
        bit = 3 << (k - 1) if k == BITS else 1 << k
        other = swap(rest, bit), swap(gram, bit)
        gram, rest = gram + other[1], rest + other[0]
    next_gram = lax.ppermute(gram, "fold", [(i, i ^ 1) for i in range(folds)])
    next_gram, rest = lax.optimization_barrier((next_gram, rest))
    even = lax.axis_index("fold") & 1 == 0
    first = jnp.where(even, gram[:gram_rows], next_gram[:gram_rows])
    second = jnp.where(even, next_gram[:gram_rows], gram[:gram_rows])
    own = jnp.concatenate([first, second, gram[gram_rows:] + next_gram[gram_rows:], rest])
    mine = jnp.concatenate([own] + [swap(own, bit) for bit in SQUARE])
    return mine, swap(mine, 1)


def pin(x):
    return pltpu.with_memory_space_constraint(x, pltpu.HBM)


def shards(devices, folds, volumes, record_index, fold_of, held_out, dictionary):
    records, voxels = volumes.shape
    batch = record_index.shape[0]
    atoms = dictionary.shape[1]
    grams, rest = layout(batch, atoms)
    gram_tiles, rest_tiles = (len(pairs) + len(plain) for pairs, plain in (grams[0], rest))
    slots = 1 << BITS
    part = jax.ShapeDtypeStruct((slots // 2 * ((gram_tiles + rest_tiles) * TILE // slots + SPARE), TILE), F32)
    vmem = pl.BlockSpec(memory_space=pltpu.VMEM)
    smem = pl.BlockSpec(memory_space=pltpu.SMEM)
    hbm = pl.BlockSpec(memory_space=pltpu.HBM)
    params = pltpu.CompilerParams(vmem_limit_bytes=48 << 20)
    keep, send, flipped, weight = pl.pallas_call(
        gram_kernel,
        out_shape=(part, part, jax.ShapeDtypeStruct((voxels, batch), F32), jax.ShapeDtypeStruct((batch, TILE), F32)),
        in_specs=[hbm, hbm, smem, hbm, hbm],
        out_specs=(vmem,) * 4,
        scratch_shapes=[pltpu.VMEM((1, batch), jnp.int32), pltpu.VMEM((1, records), jnp.int32),
                        pltpu.VMEM(volumes.shape, F32), pltpu.VMEM(dictionary.shape, F32),
                        pltpu.VMEM(((gram_tiles + rest_tiles) * TILE, TILE), F32),
                        pltpu.SemaphoreType.DMA((4,))],
        compiler_params=params,
        name="grams",
    )(pin(record_index[None]), pin(fold_of[None]), held_out, pin(volumes), pin(dictionary))
    mine, other = all_reduce(keep, send, gram_tiles * TILE // slots, devices, folds)
    outs = [dictionary.shape, (batch, atoms), (atoms, atoms)]
    return pl.pallas_call(
        step_kernel,
        out_shape=tuple(jax.ShapeDtypeStruct(shape, F32) for shape in outs),
        in_specs=[vmem] * 5,
        out_specs=(hbm,) * 3,
        scratch_shapes=[pltpu.VMEM((batch + atoms, batch + atoms), F32), pltpu.VMEM(((batch + atoms) // 2, TILE), F32)]
        + [pltpu.VMEM(shape, F32) for shape in outs] + [pltpu.SemaphoreType.DMA((5,))],
        compiler_params=params,
        name="step",
    )(mine, other, flipped, weight, dictionary)


def solution(mesh):
    in_specs = (P("fold", "vox"), P("fold"), P("fold"), P("fold"), P("vox", None))
    out_specs = (P(("fold", "vox"), None), P("fold", None), P("fold", None))
    return jax.shard_map(functools.partial(shards, mesh.shape["vox"], mesh.shape["fold"]), mesh=mesh, in_specs=in_specs, out_specs=out_specs, check_vma=False)
```

```python
import functools

import jax
import jax.numpy as jnp
from jax import lax
from jax.experimental import pallas as pl
from jax.experimental.pallas import tpu as pltpu
from jax.sharding import PartitionSpec as P

ISTA_STEPS = 5
PENALTY = 0.5
TILE = 128
SPARE = 8
BITS = 3
SQUARE = (4, 6, 2)
F32 = jnp.float32
BF16 = jnp.bfloat16

NN = (((1,), (0,)), ((), ()))
TN = (((0,), (0,)), ((), ()))
NT = (((1,), (1,)), ((), ()))


def halves(x):
    hi = x.astype(BF16)
    return hi, (x - hi.astype(F32)).astype(BF16)


def dot1(a, b, dims=NN):
    return lax.dot_general(a, b, dims, preferred_element_type=F32)


def dot3(a, b, dims=NN):
    (left,), _ = dims[0]
    rows = a[0].shape[1 - left]
    both = dot1(jnp.concatenate(a, axis=1 - left), b[0], dims)
    return both[:rows] + (both[rows:] + dot1(a[0], b[1], dims))


def square3(a, b, dims=NN):
    mixed = dot1(a[0], b[1], dims)
    return dot1(a[0], b[0], dims) + (mixed + mixed.T)


def top_row_sum(x):
    return jnp.max(jnp.sum(jnp.abs(x), axis=1, keepdims=True), axis=0, keepdims=True)


def upper_tiles(first, count):
    ends = range(first, first + count)
    return [(r, c) for r in ends for c in ends if c > r], [(r, r + 1) for r in ends[::2]]


def layout(batch, atoms):
    edge, wide = batch // TILE, atoms // TILE
    grams = []
    for fold in range(2):
        plain, pairs = upper_tiles(edge + fold * wide // 2, wide // 2)
        strip = range(edge + fold * wide // 4, edge + (fold + 1) * wide // 4)
        plain = plain + [(r, c) for r in strip for c in range(edge + wide // 2, edge + wide)]
        grams.append((pairs, plain))
    plain, pairs = upper_tiles(0, edge)
    rest = (pairs, plain + [(r, c) for r in range(edge) for c in range(edge, edge + wide)])
    return grams, rest


def slot_of(vox):
    x = (vox >> 1) & 1
    z = ((vox >> 2) ^ (vox >> 3)) & 1
    return (vox & 1) * 4 + x * 2 + (x ^ z)


def column(row):
    return jnp.broadcast_to(row, (TILE, row.shape[1])).T[:, :1]


def eye_tile():
    rows = lax.broadcasted_iota(jnp.int32, (TILE, TILE), 0)
    columns = lax.broadcasted_iota(jnp.int32, (TILE, TILE), 1)
    return rows, columns


def pack(pairs, plain, block, first, stage, at):
    rows, columns = eye_tile()

    def tile(r, c):
        r, c = (r - first[0]) * TILE, (c - first[1]) * TILE
        return block[r:r + TILE, c:c + TILE]

    apart = []
    for one, other in pairs:
        low = tile(other, other)
        stage[at * TILE:(at + 1) * TILE, :] = jnp.where(rows <= columns, tile(one, one), low)
        apart.append(jnp.sum(jnp.where(rows == columns, low, 0.0), axis=0, keepdims=True))
        at += 1
    for r, c in plain:
        stage[at * TILE:(at + 1) * TILE, :] = tile(r, c)
        at += 1
    return apart, at


def gram_kernel(index_hbm, fold_hbm, held_ref, volumes_hbm, dict_hbm,
                keep_ref, send_ref, flipped_ref, weight_ref, index_ref, fold_ref, volumes_ref, dict_ref, stage, sems):
    pairs = ((index_hbm, index_ref), (fold_hbm, fold_ref), (volumes_hbm, volumes_ref), (dict_hbm, dict_ref))
    copies = [pltpu.make_async_copy(source, target, sems.at[j]) for j, (source, target) in enumerate(pairs)]
    for copy in copies:
        copy.start()
    batch = index_ref.shape[1]
    records = volumes_ref.shape[0]
    atoms = dict_ref.shape[1]
    edge = batch // TILE
    wide = atoms // TILE
    grams, (rest_pairs, rest_plain) = layout(batch, atoms)
    fold = lax.axis_index("fold") & 1
    for copy in copies[:-1]:
        copy.wait()
    pick = lax.broadcasted_iota(jnp.int32, (records, batch), 0) == index_ref[...]
    pick = pick.astype(F32).astype(BF16)
    v = halves(volumes_ref[...])
    b = (dot1(pick, v[0], TN), dot1(pick, v[1], TN))
    flipped_ref[...] = (b[0] + b[1]).T
    b = (b[0].astype(BF16), b[1].astype(BF16))
    copies[-1].wait()
    d = halves(dict_ref[...])
    far = slice(atoms // 2, atoms)
    mine = halves(dict_ref[:, pl.ds(pl.multiple_of(fold * (atoms // 2), TILE), atoms // 2)])
    strip = halves(dict_ref[:, pl.ds(pl.multiple_of(fold * (atoms // 4), TILE), atoms // 4)])
    near, plain = grams[0]
    apart, at = pack(near, [t for t in plain if t[1] < edge + wide // 2], square3(mine, mine, TN), (edge, edge), stage, 0)
    _, at = pack([], [t for t in plain if t[1] >= edge + wide // 2],
                 dot3(strip, (d[0][:, far], d[1][:, far]), TN), (edge, edge + wide // 2), stage, at)
    first = at
    own, at = pack(rest_pairs, [t for t in rest_plain if t[1] < edge], square3(b, b, NT), (0, 0), stage, at)
    _, at = pack([], [t for t in rest_plain if t[1] >= edge], dot3(b, d), (0, edge), stage, at)
    folds = jnp.broadcast_to(fold_ref[...], (TILE, records)).astype(F32).astype(BF16)
    folds = dot1(pick, folds, (((0,), (1,)), ((), ())))
    weight_ref[...] = jnp.where(folds != held_ref[0].astype(F32), 1.0, 0.0)

    place = lax.broadcasted_iota(jnp.int32, (SPARE, TILE), 0) - fold * (SPARE // 2)
    spare = jnp.zeros((SPARE, TILE), F32)
    for j, row in enumerate(apart + own):
        spare = spare + jnp.where(place == j, row, 0.0)
    slots = 1 << BITS
    rows = TILE // slots
    me = slot_of(lax.axis_index("vox"))
    half = slots // 2
    for o in range(slots):
        out = keep_ref if o < half else send_ref
        which = me ^ o
        base = o % half * (at * rows + SPARE)
        for k in range(at):
            to = base + k * rows + (SPARE if k >= first else 0)
            out[to:to + rows, :] = stage[pl.ds(pl.multiple_of(k * TILE + which * rows, rows), rows), :]
        out[base + first * rows:base + first * rows + SPARE, :] = jnp.where(which == 0, spare, 0.0)


def step_kernel(mine_ref, other_ref, flipped_ref, weight_ref, dict_ref,
                new_hbm, code_hbm, gram_hbm, full, stage, new_ref, code_ref, gram_ref, sems):
    batch = flipped_ref.shape[1]
    voxels, atoms = dict_ref.shape
    slots = 1 << BITS
    rows = TILE // slots
    half = slots // 2
    place = slot_of(lax.axis_index("vox"))
    grams, rest = layout(batch, atoms)
    kinds = []
    for pairs, plain in grams + [rest]:
        kinds += [(pair, True) for pair in pairs] + [(tile, False) for tile in plain]
    split = len(kinds) - len(rest[0]) - len(rest[1])
    spare = jnp.zeros((SPARE, TILE), F32)
    for o in range(slots):
        source = mine_ref if o < half else other_ref
        start = (place ^ o) * rows
        base = o % half * (len(kinds) * rows + SPARE)
        packed = 0
        for k, ((r, c), pair) in enumerate(kinds):
            at = base + k * rows + (SPARE if k >= split else 0)
            value = source[at:at + rows, :]
            if pair:
                stage[pl.ds(pl.multiple_of(packed * TILE + start, rows), rows), :] = value
                packed += 1
            else:
                full[pl.ds(pl.multiple_of(r * TILE + start, rows), rows), c * TILE:(c + 1) * TILE] = value
        spare = spare + source[base + split * rows:base + split * rows + SPARE, :]
    across, down = eye_tile()
    own = len(grams[0][0])
    mate = lax.axis_index("fold") & 1
    packed = 0
    for k, ((r, c), pair) in enumerate(kinds):
        if pair:
            value = stage[packed * TILE:(packed + 1) * TILE, :]
            turned = value.T
            if packed < 2 * own:
                at = packed // own * (SPARE // 2) + packed % own
                diagonal = spare[at:at + 1, :]
            else:
                at = own + packed - 2 * own
                diagonal = jnp.where(mate == 0, spare[at:at + 1, :], spare[at + SPARE // 2:at + SPARE // 2 + 1, :])
            packed += 1
            full[r * TILE:(r + 1) * TILE, r * TILE:(r + 1) * TILE] = jnp.where(across <= down, value, turned)
            full[c * TILE:(c + 1) * TILE, c * TILE:(c + 1) * TILE] = jnp.where(
                across == down, diagonal, jnp.where(across > down, value, turned))
        elif r * TILE >= batch or c * TILE < batch:
            full[c * TILE:(c + 1) * TILE, r * TILE:(r + 1) * TILE] = full[r * TILE:(r + 1) * TILE, c * TILE:(c + 1) * TILE].T

    gram = full[batch:, batch:]
    bound = top_row_sum(gram)
    inverse = 1.0 / bound
    limit = PENALTY * inverse
    g = halves(gram)
    corr = full[:batch, batch:]
    moved = corr * inverse
    code = moved - jnp.clip(moved, -limit, limit)
    groups = [slice(0, batch // 2), slice(batch // 2, batch)]
    codes = [code[group] for group in groups]
    for _ in range(ISTA_STEPS - 1):
        for j, group in enumerate(groups):
            moved = codes[j] - (dot3(halves(codes[j]), g) - corr[group]) * inverse
            codes[j] = moved - jnp.clip(moved, -limit, limit)
    code = jnp.concatenate(codes, axis=0)
    code_ref[...] = code
    code_copy = pltpu.make_async_copy(code_ref, code_hbm, sems.at[0])
    code_copy.start()

    x = halves(code)
    weighted = code * jnp.concatenate([weight_ref[...]] * (atoms // TILE), axis=1)
    w = halves(weighted)
    turned_w = halves(weighted.T)
    fit = corr - dot3(x, g)

    def residuals(corr_now, now):
        both = dot3(halves(jnp.concatenate([corr_now, now], axis=0)), x, NT)
        return full[:batch, :batch] - both[:batch], flipped_ref[...] - both[batch:]

    cross, rest = residuals(corr, dict_ref[...])
    step = 1.0 / (1.0 + top_row_sum(square3(turned_w, w)))
    square = cross - dot3(x, halves(fit), NT)
    tile_eye = across == down
    squares = jnp.concatenate(
        [jnp.sum(jnp.where(tile_eye, gram[r:r + TILE, r:r + TILE], 0.0), axis=0, keepdims=True)
         for r in range(0, atoms, TILE)], axis=1)
    moves = dot3(halves(jnp.concatenate([square, cross, rest], axis=0)), w)
    change = fit + (0.5 * step) * moves[:batch]
    squares = squares + 2.0 * step * jnp.sum(weighted * change, axis=0, keepdims=True)
    scale = 1.0 / jnp.sqrt(jnp.maximum(squares, 1.0))
    outer = dot3(turned_w, halves(change))
    corr = (corr + step * moves[batch:2 * batch]) * scale
    now = (dict_ref[...] + step * moves[2 * batch:]) * scale
    new_ref[...] = now
    cross, rest = residuals(corr, now)
    gram = (gram + step * (outer + outer.T)) * scale * column(scale)
    fit = corr - dot3(x, halves(gram))
    square = cross - dot3(x, halves(fit), NT)
    squares = squares * scale * scale
    moves = dot3(halves(jnp.concatenate([square, rest], axis=0)), w)
    change = fit + (0.5 * step) * moves[:batch]
    squares = squares + 2.0 * step * jnp.sum(weighted * change, axis=0, keepdims=True)
    scale = 1.0 / jnp.sqrt(jnp.maximum(squares, 1.0))
    copies = [code_copy]
    block = voxels // 3 if voxels % 3 == 0 and (voxels // 3) % 16 == 0 else voxels
    for j in range(voxels // block):
        here = slice(j * block, (j + 1) * block)
        new_ref[here, :] = (new_ref[here, :] + step * moves[batch + j * block:batch + (j + 1) * block]) * scale
        copies.append(pltpu.make_async_copy(new_ref.at[here, :], new_hbm.at[here, :], sems.at[2 + j]))
        copies[-1].start()
    outer = dot3(turned_w, halves(change))
    gram_ref[...] = (gram + step * (outer + outer.T)) * scale * column(scale)
    copies.append(pltpu.make_async_copy(gram_ref, gram_hbm, sems.at[1]))
    copies[-1].start()
    for copy in copies:
        copy.wait()


def all_reduce(keep, send, gram_rows, devices, folds):
    def swap(x, bit):
        return lax.ppermute(x, "vox", [(i, i ^ bit) for i in range(devices)])

    total = keep + swap(send, 1)
    slot = total.shape[0] // (len(SQUARE) + 1)
    own = total[:slot]
    got = [swap(total[(k + 1) * slot:(k + 2) * slot], bit) for k, bit in enumerate(SQUARE)]
    for part in got:
        own = own + part
    head = gram_rows + SPARE
    cut = max(head, -(-own.shape[0] // 16) * 8)
    gram, rest = lax.optimization_barrier((own[:cut], own[cut:]))
    for k in range(BITS, devices.bit_length() - 1):
        bit = 3 << (k - 1) if k == BITS else 1 << k
        other = swap(gram, bit), swap(rest, bit)
        gram, rest = gram + other[0], rest + other[1]
    next_gram = lax.ppermute(gram[:head], "fold", [(i, i ^ 1) for i in range(folds)])
    next_gram, rest = lax.optimization_barrier((next_gram, rest))
    even = lax.axis_index("fold") & 1 == 0
    first = jnp.where(even, gram[:gram_rows], next_gram[:gram_rows])
    second = jnp.where(even, next_gram[:gram_rows], gram[:gram_rows])
    own = jnp.concatenate([first, second, gram[gram_rows:head] + next_gram[gram_rows:], gram[head:], rest])
    ahead, across, along = (swap(own, bit) for bit in SQUARE)
    across, along, ahead = lax.optimization_barrier((across, along, ahead))
    mine = jnp.concatenate([own, ahead, across, along])
    return mine, swap(mine, 1)


def pin(x):
    return pltpu.with_memory_space_constraint(x, pltpu.HBM)


def shards(devices, folds, volumes, record_index, fold_of, held_out, dictionary):
    records, voxels = volumes.shape
    batch = record_index.shape[0]
    atoms = dictionary.shape[1]
    grams, rest = layout(batch, atoms)
    gram_tiles, rest_tiles = (len(pairs) + len(plain) for pairs, plain in (grams[0], rest))
    slots = 1 << BITS
    part = jax.ShapeDtypeStruct((slots // 2 * ((gram_tiles + rest_tiles) * TILE // slots + SPARE), TILE), F32)
    vmem = pl.BlockSpec(memory_space=pltpu.VMEM)
    smem = pl.BlockSpec(memory_space=pltpu.SMEM)
    hbm = pl.BlockSpec(memory_space=pltpu.HBM)
    params = pltpu.CompilerParams(vmem_limit_bytes=48 << 20)
    keep, send, flipped, weight = pl.pallas_call(
        gram_kernel,
        out_shape=(part, part, jax.ShapeDtypeStruct((voxels, batch), F32), jax.ShapeDtypeStruct((batch, TILE), F32)),
        in_specs=[hbm, hbm, smem, hbm, hbm],
        out_specs=(vmem,) * 4,
        scratch_shapes=[pltpu.VMEM((1, batch), jnp.int32), pltpu.VMEM((1, records), jnp.int32),
                        pltpu.VMEM(volumes.shape, F32), pltpu.VMEM(dictionary.shape, F32),
                        pltpu.VMEM(((gram_tiles + rest_tiles) * TILE, TILE), F32),
                        pltpu.SemaphoreType.DMA((4,))],
        compiler_params=params,
        name="grams",
    )(pin(record_index[None]), pin(fold_of[None]), held_out, pin(volumes), pin(dictionary))
    mine, other = all_reduce(keep, send, gram_tiles * TILE // slots, devices, folds)
    outs = [dictionary.shape, (batch, atoms), (atoms, atoms)]
    return pl.pallas_call(
        step_kernel,
        out_shape=tuple(jax.ShapeDtypeStruct(shape, F32) for shape in outs),
        in_specs=[vmem] * 5,
        out_specs=(hbm,) * 3,
        scratch_shapes=[pltpu.VMEM((batch + atoms, batch + atoms), F32), pltpu.VMEM(((batch + atoms) // 2, TILE), F32)]
        + [pltpu.VMEM(shape, F32) for shape in outs] + [pltpu.SemaphoreType.DMA((5,))],
        compiler_params=params,
        name="step",
    )(mine, other, flipped, weight, dictionary)


def solution(mesh):
    in_specs = (P("fold", "vox"), P("fold"), P("fold"), P("fold"), P("vox", None))
    out_specs = (P(("fold", "vox"), None), P("fold", None), P("fold", None))
    return jax.shard_map(functools.partial(shards, mesh.shape["vox"], mesh.shape["fold"]), mesh=mesh, in_specs=in_specs, out_specs=out_specs, check_vma=False)
```

```python
import functools

import jax
import jax.numpy as jnp
from jax import lax
from jax.experimental import pallas as pl
from jax.experimental.pallas import tpu as pltpu
from jax.sharding import PartitionSpec as P

ISTA_STEPS = 5
PENALTY = 0.5
TILE = 128
SPARE = 8
BITS = 3
SQUARE = (4, 6, 2)
F32 = jnp.float32
BF16 = jnp.bfloat16

NN = (((1,), (0,)), ((), ()))
TN = (((0,), (0,)), ((), ()))
NT = (((1,), (1,)), ((), ()))


def halves(x):
    hi = x.astype(BF16)
    return hi, (x - hi.astype(F32)).astype(BF16)


def dot1(a, b, dims=NN):
    return lax.dot_general(a, b, dims, preferred_element_type=F32)


def dot3(a, b, dims=NN):
    (left,), _ = dims[0]
    rows = a[0].shape[1 - left]
    both = dot1(jnp.concatenate(a, axis=1 - left), b[0], dims)
    return both[:rows] + (both[rows:] + dot1(a[0], b[1], dims))


def square3(a, b, dims=NN):
    mixed = dot1(a[0], b[1], dims)
    return dot1(a[0], b[0], dims) + (mixed + mixed.T)


def top_row_sum(x):
    return jnp.max(jnp.sum(jnp.abs(x), axis=1, keepdims=True), axis=0, keepdims=True)


def upper_tiles(first, count):
    ends = range(first, first + count)
    return [(r, c) for r in ends for c in ends if c > r], [(r, r + 1) for r in ends[::2]]


def layout(batch, atoms):
    edge, wide = batch // TILE, atoms // TILE
    grams = []
    for fold in range(2):
        plain, pairs = upper_tiles(edge + fold * wide // 2, wide // 2)
        strip = range(edge + fold * wide // 4, edge + (fold + 1) * wide // 4)
        plain = plain + [(r, c) for r in strip for c in range(edge + wide // 2, edge + wide)]
        grams.append((pairs, plain))
    plain, pairs = upper_tiles(0, edge)
    rest = (pairs, plain + [(r, c) for r in range(edge) for c in range(edge, edge + wide)])
    return grams, rest


def slot_of(vox):
    x = (vox >> 1) & 1
    z = ((vox >> 2) ^ (vox >> 3)) & 1
    return (vox & 1) * 4 + x * 2 + (x ^ z)


def column(row):
    return jnp.broadcast_to(row, (TILE, row.shape[1])).T[:, :1]


def eye_tile():
    rows = lax.broadcasted_iota(jnp.int32, (TILE, TILE), 0)
    columns = lax.broadcasted_iota(jnp.int32, (TILE, TILE), 1)
    return rows, columns


def pack(pairs, plain, block, first, stage, at):
    rows, columns = eye_tile()

    def tile(r, c):
        r, c = (r - first[0]) * TILE, (c - first[1]) * TILE
        return block[r:r + TILE, c:c + TILE]

    apart = []
    for one, other in pairs:
        low = tile(other, other)
        stage[at * TILE:(at + 1) * TILE, :] = jnp.where(rows <= columns, tile(one, one), low)
        apart.append(jnp.sum(jnp.where(rows == columns, low, 0.0), axis=0, keepdims=True))
        at += 1
    for r, c in plain:
        stage[at * TILE:(at + 1) * TILE, :] = tile(r, c)
        at += 1
    return apart, at


def gram_kernel(index_hbm, fold_hbm, held_ref, volumes_hbm, dict_hbm,
                keep_ref, send_ref, flipped_ref, weight_ref, index_ref, fold_ref, volumes_ref, dict_ref, stage, sems):
    pairs = ((index_hbm, index_ref), (fold_hbm, fold_ref), (volumes_hbm, volumes_ref), (dict_hbm, dict_ref))
    copies = [pltpu.make_async_copy(source, target, sems.at[j]) for j, (source, target) in enumerate(pairs)]
    for copy in copies:
        copy.start()
    batch = index_ref.shape[1]
    records = volumes_ref.shape[0]
    atoms = dict_ref.shape[1]
    edge = batch // TILE
    wide = atoms // TILE
    grams, (rest_pairs, rest_plain) = layout(batch, atoms)
    fold = lax.axis_index("fold") & 1
    for copy in copies[:-1]:
        copy.wait()
    pick = lax.broadcasted_iota(jnp.int32, (records, batch), 0) == index_ref[...]
    pick = pick.astype(F32).astype(BF16)
    v = halves(volumes_ref[...])
    b = (dot1(pick, v[0], TN), dot1(pick, v[1], TN))
    flipped_ref[...] = (b[0] + b[1]).T
    b = (b[0].astype(BF16), b[1].astype(BF16))
    copies[-1].wait()
    d = halves(dict_ref[...])
    far = slice(atoms // 2, atoms)
    mine = halves(dict_ref[:, pl.ds(pl.multiple_of(fold * (atoms // 2), TILE), atoms // 2)])
    strip = halves(dict_ref[:, pl.ds(pl.multiple_of(fold * (atoms // 4), TILE), atoms // 4)])
    near, plain = grams[0]
    apart, at = pack(near, [t for t in plain if t[1] < edge + wide // 2], square3(mine, mine, TN), (edge, edge), stage, 0)
    _, at = pack([], [t for t in plain if t[1] >= edge + wide // 2],
                 dot3(strip, (d[0][:, far], d[1][:, far]), TN), (edge, edge + wide // 2), stage, at)
    first = at
    own, at = pack(rest_pairs, [t for t in rest_plain if t[1] < edge], square3(b, b, NT), (0, 0), stage, at)
    _, at = pack([], [t for t in rest_plain if t[1] >= edge], dot3(b, d), (0, edge), stage, at)
    folds = jnp.broadcast_to(fold_ref[...], (TILE, records)).astype(F32).astype(BF16)
    folds = dot1(pick, folds, (((0,), (1,)), ((), ())))
    weight_ref[...] = jnp.where(folds != held_ref[0].astype(F32), 1.0, 0.0)

    place = lax.broadcasted_iota(jnp.int32, (SPARE, TILE), 0) - fold * (SPARE // 2)
    spare = jnp.zeros((SPARE, TILE), F32)
    for j, row in enumerate(apart + own):
        spare = spare + jnp.where(place == j, row, 0.0)
    slots = 1 << BITS
    rows = TILE // slots
    me = slot_of(lax.axis_index("vox"))
    half = slots // 2
    for o in range(slots):
        out = keep_ref if o < half else send_ref
        which = me ^ o
        base = o % half * (at * rows + SPARE)
        for k in range(at):
            to = base + k * rows + (SPARE if k >= first else 0)
            out[to:to + rows, :] = stage[pl.ds(pl.multiple_of(k * TILE + which * rows, rows), rows), :]
        out[base + first * rows:base + first * rows + SPARE, :] = jnp.where(which == 0, spare, 0.0)


def step_kernel(mine_ref, other_ref, flipped_ref, weight_ref, dict_ref,
                new_hbm, code_hbm, gram_hbm, full, stage, new_ref, code_ref, gram_ref, sems):
    batch = flipped_ref.shape[1]
    voxels, atoms = dict_ref.shape
    slots = 1 << BITS
    rows = TILE // slots
    half = slots // 2
    place = slot_of(lax.axis_index("vox"))
    grams, rest = layout(batch, atoms)
    kinds = []
    for pairs, plain in grams + [rest]:
        kinds += [(pair, True) for pair in pairs] + [(tile, False) for tile in plain]
    split = len(kinds) - len(rest[0]) - len(rest[1])
    spare = jnp.zeros((SPARE, TILE), F32)
    for o in range(slots):
        source = mine_ref if o < half else other_ref
        start = (place ^ o) * rows
        base = o % half * (len(kinds) * rows + SPARE)
        packed = 0
        for k, ((r, c), pair) in enumerate(kinds):
            at = base + k * rows + (SPARE if k >= split else 0)
            value = source[at:at + rows, :]
            if pair:
                stage[pl.ds(pl.multiple_of(packed * TILE + start, rows), rows), :] = value
                packed += 1
            else:
                full[pl.ds(pl.multiple_of(r * TILE + start, rows), rows), c * TILE:(c + 1) * TILE] = value
        spare = spare + source[base + split * rows:base + split * rows + SPARE, :]
    across, down = eye_tile()
    own = len(grams[0][0])
    mate = lax.axis_index("fold") & 1
    packed = 0
    for k, ((r, c), pair) in enumerate(kinds):
        if pair:
            value = stage[packed * TILE:(packed + 1) * TILE, :]
            turned = value.T
            if packed < 2 * own:
                at = packed // own * (SPARE // 2) + packed % own
                diagonal = spare[at:at + 1, :]
            else:
                at = own + packed - 2 * own
                diagonal = jnp.where(mate == 0, spare[at:at + 1, :], spare[at + SPARE // 2:at + SPARE // 2 + 1, :])
            packed += 1
            full[r * TILE:(r + 1) * TILE, r * TILE:(r + 1) * TILE] = jnp.where(across <= down, value, turned)
            full[c * TILE:(c + 1) * TILE, c * TILE:(c + 1) * TILE] = jnp.where(
                across == down, diagonal, jnp.where(across > down, value, turned))
        elif r * TILE >= batch or c * TILE < batch:
            full[c * TILE:(c + 1) * TILE, r * TILE:(r + 1) * TILE] = full[r * TILE:(r + 1) * TILE, c * TILE:(c + 1) * TILE].T

    gram = full[batch:, batch:]
    bound = top_row_sum(gram)
    inverse = 1.0 / bound
    limit = PENALTY * inverse
    g = halves(gram)
    corr = full[:batch, batch:]
    moved = corr * inverse
    code = moved - jnp.clip(moved, -limit, limit)
    groups = [slice(0, batch // 2), slice(batch // 2, batch)]
    codes = [code[group] for group in groups]
    for _ in range(ISTA_STEPS - 1):
        for j, group in enumerate(groups):
            moved = codes[j] - (dot3(halves(codes[j]), g) - corr[group]) * inverse
            codes[j] = moved - jnp.clip(moved, -limit, limit)
    code = jnp.concatenate(codes, axis=0)
    code_ref[...] = code
    code_copy = pltpu.make_async_copy(code_ref, code_hbm, sems.at[0])
    code_copy.start()

    x = halves(code)
    weighted = code * jnp.concatenate([weight_ref[...]] * (atoms // TILE), axis=1)
    w = halves(weighted)
    turned_w = halves(weighted.T)
    fit = corr - dot3(x, g)

    def residuals(corr_now, now):
        both = dot3(halves(jnp.concatenate([corr_now, now], axis=0)), x, NT)
        return full[:batch, :batch] - both[:batch], flipped_ref[...] - both[batch:]

    cross, rest = residuals(corr, dict_ref[...])
    step = 1.0 / (1.0 + top_row_sum(square3(turned_w, w)))
    square = cross - dot3(x, halves(fit), NT)
    tile_eye = across == down
    squares = jnp.concatenate(
        [jnp.sum(jnp.where(tile_eye, gram[r:r + TILE, r:r + TILE], 0.0), axis=0, keepdims=True)
         for r in range(0, atoms, TILE)], axis=1)
    moves = dot3(halves(jnp.concatenate([square, cross, rest], axis=0)), w)
    change = fit + (0.5 * step) * moves[:batch]
    squares = squares + 2.0 * step * jnp.sum(weighted * change, axis=0, keepdims=True)
    scale = 1.0 / jnp.sqrt(jnp.maximum(squares, 1.0))
    outer = dot3(turned_w, halves(change))
    corr = (corr + step * moves[batch:2 * batch]) * scale
    now = (dict_ref[...] + step * moves[2 * batch:]) * scale
    new_ref[...] = now
    cross, rest = residuals(corr, now)
    gram = (gram + step * (outer + outer.T)) * scale * column(scale)
    fit = corr - dot3(x, halves(gram))
    square = cross - dot3(x, halves(fit), NT)
    squares = squares * scale * scale
    moves = dot3(halves(jnp.concatenate([square, rest], axis=0)), w)
    change = fit + (0.5 * step) * moves[:batch]
    squares = squares + 2.0 * step * jnp.sum(weighted * change, axis=0, keepdims=True)
    scale = 1.0 / jnp.sqrt(jnp.maximum(squares, 1.0))
    copies = [code_copy]
    block = voxels // 3 if voxels % 3 == 0 and (voxels // 3) % 16 == 0 else voxels
    for j in range(voxels // block):
        here = slice(j * block, (j + 1) * block)
        new_ref[here, :] = (new_ref[here, :] + step * moves[batch + j * block:batch + (j + 1) * block]) * scale
        copies.append(pltpu.make_async_copy(new_ref.at[here, :], new_hbm.at[here, :], sems.at[2 + j]))
        copies[-1].start()
    outer = dot3(turned_w, halves(change))
    gram_ref[...] = (gram + step * (outer + outer.T)) * scale * column(scale)
    copies.append(pltpu.make_async_copy(gram_ref, gram_hbm, sems.at[1]))
    copies[-1].start()
    for copy in copies:
        copy.wait()


def all_reduce(keep, send, gram_rows, devices, folds):
    def swap(x, bit):
        return lax.ppermute(x, "vox", [(i, i ^ bit) for i in range(devices)])

    total = keep + swap(send, 1)
    slot = total.shape[0] // (len(SQUARE) + 1)
    own = total[:slot]
    got = [swap(total[(k + 1) * slot:(k + 2) * slot], bit) for k, bit in enumerate(SQUARE)]
    for part in got:
        own = own + part
    head = gram_rows + SPARE
    cut = head + 2 * SPARE
    gram, rest = lax.optimization_barrier((own[:cut], own[cut:]))
    for k in range(BITS, devices.bit_length() - 1):
        bit = 3 << (k - 1) if k == BITS else 1 << k
        other = swap(gram, bit), swap(rest, bit)
        gram, rest = gram + other[0], rest + other[1]
    next_gram = lax.ppermute(gram[:head], "fold", [(i, i ^ 1) for i in range(folds)])
    next_gram, rest = lax.optimization_barrier((next_gram, rest))
    even = lax.axis_index("fold") & 1 == 0
    first = jnp.where(even, gram[:gram_rows], next_gram[:gram_rows])
    second = jnp.where(even, next_gram[:gram_rows], gram[:gram_rows])
    own = jnp.concatenate([first, second, gram[gram_rows:head] + next_gram[gram_rows:], gram[head:], rest])
    ahead, across, along = (swap(own, bit) for bit in SQUARE)
    across, along, ahead = lax.optimization_barrier((across, along, ahead))
    mine = jnp.concatenate([own, ahead, across, along])
    return mine, swap(mine, 1)


def pin(x):
    return pltpu.with_memory_space_constraint(x, pltpu.HBM)


def shards(devices, folds, volumes, record_index, fold_of, held_out, dictionary):
    records, voxels = volumes.shape
    batch = record_index.shape[0]
    atoms = dictionary.shape[1]
    grams, rest = layout(batch, atoms)
    gram_tiles, rest_tiles = (len(pairs) + len(plain) for pairs, plain in (grams[0], rest))
    slots = 1 << BITS
    part = jax.ShapeDtypeStruct((slots // 2 * ((gram_tiles + rest_tiles) * TILE // slots + SPARE), TILE), F32)
    vmem = pl.BlockSpec(memory_space=pltpu.VMEM)
    smem = pl.BlockSpec(memory_space=pltpu.SMEM)
    hbm = pl.BlockSpec(memory_space=pltpu.HBM)
    params = pltpu.CompilerParams(vmem_limit_bytes=48 << 20)
    keep, send, flipped, weight = pl.pallas_call(
        gram_kernel,
        out_shape=(part, part, jax.ShapeDtypeStruct((voxels, batch), F32), jax.ShapeDtypeStruct((batch, TILE), F32)),
        in_specs=[hbm, hbm, smem, hbm, hbm],
        out_specs=(vmem,) * 4,
        scratch_shapes=[pltpu.VMEM((1, batch), jnp.int32), pltpu.VMEM((1, records), jnp.int32),
                        pltpu.VMEM(volumes.shape, F32), pltpu.VMEM(dictionary.shape, F32),
                        pltpu.VMEM(((gram_tiles + rest_tiles) * TILE, TILE), F32),
                        pltpu.SemaphoreType.DMA((4,))],
        compiler_params=params,
        name="grams",
    )(pin(record_index[None]), pin(fold_of[None]), held_out, pin(volumes), pin(dictionary))
    mine, other = all_reduce(keep, send, gram_tiles * TILE // slots, devices, folds)
    outs = [dictionary.shape, (batch, atoms), (atoms, atoms)]
    return pl.pallas_call(
        step_kernel,
        out_shape=tuple(jax.ShapeDtypeStruct(shape, F32) for shape in outs),
        in_specs=[vmem] * 5,
        out_specs=(hbm,) * 3,
        scratch_shapes=[pltpu.VMEM((batch + atoms, batch + atoms), F32), pltpu.VMEM(((batch + atoms) // 2, TILE), F32)]
        + [pltpu.VMEM(shape, F32) for shape in outs] + [pltpu.SemaphoreType.DMA((5,))],
        compiler_params=params,
        name="step",
    )(mine, other, flipped, weight, dictionary)


def solution(mesh):
    in_specs = (P("fold", "vox"), P("fold"), P("fold"), P("fold"), P("vox", None))
    out_specs = (P(("fold", "vox"), None), P("fold", None), P("fold", None))
    return jax.shard_map(functools.partial(shards, mesh.shape["vox"], mesh.shape["fold"]), mesh=mesh, in_specs=in_specs, out_specs=out_specs, check_vma=False)
```

```python
import functools

import jax
import jax.numpy as jnp
from jax import lax
from jax.experimental import pallas as pl
from jax.experimental.pallas import tpu as pltpu
from jax.sharding import PartitionSpec as P

ISTA_STEPS = 5
PENALTY = 0.5
TILE = 128
SPARE = 8
BITS = 3
SQUARE = ((4, 2), (6, 6), (2, 4))
F32 = jnp.float32
BF16 = jnp.bfloat16

NN = (((1,), (0,)), ((), ()))
TN = (((0,), (0,)), ((), ()))
NT = (((1,), (1,)), ((), ()))


def halves(x):
    hi = x.astype(BF16)
    return hi, (x - hi.astype(F32)).astype(BF16)


def dot1(a, b, dims=NN):
    return lax.dot_general(a, b, dims, preferred_element_type=F32)


def dot3(a, b, dims=NN):
    (left,), _ = dims[0]
    rows = a[0].shape[1 - left]
    both = dot1(jnp.concatenate(a, axis=1 - left), b[0], dims)
    return both[:rows] + (both[rows:] + dot1(a[0], b[1], dims))


def square3(a, b, dims=NN):
    mixed = dot1(a[0], b[1], dims)
    return dot1(a[0], b[0], dims) + (mixed + mixed.T)


def top_row_sum(x):
    return jnp.max(jnp.sum(jnp.abs(x), axis=0, keepdims=True), axis=1, keepdims=True)


def upper_tiles(first, count):
    ends = range(first, first + count)
    return [(r, c) for r in ends for c in ends if c > r], [(r, r + 1) for r in ends[::2]]


def layout(batch, atoms):
    edge, wide = batch // TILE, atoms // TILE
    grams = []
    for fold in range(2):
        plain, pairs = upper_tiles(edge + fold * wide // 2, wide // 2)
        strip = range(edge + fold * wide // 4, edge + (fold + 1) * wide // 4)
        plain = plain + [(r, c) for r in strip for c in range(edge + wide // 2, edge + wide)]
        grams.append((pairs, plain))
    plain, pairs = upper_tiles(0, edge)
    rest = (pairs, plain + [(r, c) for r in range(edge) for c in range(edge, edge + wide)])
    return grams, rest


def slot_of(vox):
    core = vox & 1
    x = (vox >> 1) & 1
    z = ((vox >> 2) ^ (vox >> 3)) & 1
    return core * 4 + (x + core * (z - x)) * 2 + (x ^ z)


def column(row):
    return jnp.broadcast_to(row, (TILE, row.shape[1])).T[:, :1]


def eye_tile():
    rows = lax.broadcasted_iota(jnp.int32, (TILE, TILE), 0)
    columns = lax.broadcasted_iota(jnp.int32, (TILE, TILE), 1)
    return rows, columns


def pack(pairs, plain, block, first, stage, at):
    rows, columns = eye_tile()

    def tile(r, c):
        r, c = (r - first[0]) * TILE, (c - first[1]) * TILE
        return block[r:r + TILE, c:c + TILE]

    apart = []
    for one, other in pairs:
        low = tile(other, other)
        stage[at * TILE:(at + 1) * TILE, :] = jnp.where(rows <= columns, tile(one, one), low)
        apart.append(jnp.sum(jnp.where(rows == columns, low, 0.0), axis=0, keepdims=True))
        at += 1
    for r, c in plain:
        stage[at * TILE:(at + 1) * TILE, :] = tile(r, c)
        at += 1
    return apart, at


def gram_kernel(index_hbm, fold_hbm, held_ref, volumes_hbm, dict_hbm,
                keep_ref, send_ref, flipped_ref, weight_ref, index_ref, fold_ref, volumes_ref, dict_ref, stage, sems):
    pairs = ((index_hbm, index_ref), (fold_hbm, fold_ref), (volumes_hbm, volumes_ref), (dict_hbm, dict_ref))
    copies = [pltpu.make_async_copy(source, target, sems.at[j]) for j, (source, target) in enumerate(pairs)]
    for copy in copies:
        copy.start()
    batch = index_ref.shape[1]
    records = volumes_ref.shape[0]
    atoms = dict_ref.shape[1]
    edge = batch // TILE
    wide = atoms // TILE
    grams, (rest_pairs, rest_plain) = layout(batch, atoms)
    fold = lax.axis_index("fold") & 1
    for copy in copies[:-1]:
        copy.wait()
    pick = lax.broadcasted_iota(jnp.int32, (records, batch), 0) == index_ref[...]
    pick = pick.astype(F32).astype(BF16)
    v = halves(volumes_ref[...])
    b = (dot1(pick, v[0], TN), dot1(pick, v[1], TN))
    flipped_ref[...] = (b[0] + b[1]).T
    b = (b[0].astype(BF16), b[1].astype(BF16))
    copies[-1].wait()
    d = halves(dict_ref[...])
    far = slice(atoms // 2, atoms)
    mine = halves(dict_ref[:, pl.ds(pl.multiple_of(fold * (atoms // 2), TILE), atoms // 2)])
    strip = halves(dict_ref[:, pl.ds(pl.multiple_of(fold * (atoms // 4), TILE), atoms // 4)])
    near, plain = grams[0]
    apart, at = pack(near, [t for t in plain if t[1] < edge + wide // 2], square3(mine, mine, TN), (edge, edge), stage, 0)
    _, at = pack([], [t for t in plain if t[1] >= edge + wide // 2],
                 dot3(strip, (d[0][:, far], d[1][:, far]), TN), (edge, edge + wide // 2), stage, at)
    first = at
    own, at = pack(rest_pairs, [t for t in rest_plain if t[1] < edge], square3(b, b, NT), (0, 0), stage, at)
    _, at = pack([], [t for t in rest_plain if t[1] >= edge], dot3(b, d), (0, edge), stage, at)
    folds = jnp.broadcast_to(fold_ref[...], (TILE, records)).astype(F32).astype(BF16)
    folds = dot1(pick, folds, (((0,), (1,)), ((), ())))
    weight_ref[...] = jnp.where(folds != held_ref[0].astype(F32), 1.0, 0.0)

    place = lax.broadcasted_iota(jnp.int32, (SPARE, TILE), 0) - fold * (SPARE // 2)
    spare = jnp.zeros((SPARE, TILE), F32)
    for j, row in enumerate(apart + own):
        spare = spare + jnp.where(place == j, row, 0.0)
    slots = 1 << BITS
    rows = TILE // slots
    vox = lax.axis_index("vox")
    half = slots // 2
    for o in range(slots):
        out = keep_ref if o < half else send_ref
        which = slot_of(vox ^ (o // half)) ^ (o % half)
        base = o % half * (at * rows + SPARE)
        for k in range(at):
            to = base + k * rows + (SPARE if k >= first else 0)
            out[to:to + rows, :] = stage[pl.ds(pl.multiple_of(k * TILE + which * rows, rows), rows), :]
        out[base + first * rows:base + first * rows + SPARE, :] = jnp.where(which == 0, spare, 0.0)


def step_kernel(mine_ref, other_ref, flipped_ref, weight_ref, dict_ref,
                new_hbm, code_hbm, gram_hbm, full, stage, new_ref, code_ref, gram_ref, sems):
    batch = flipped_ref.shape[1]
    voxels, atoms = dict_ref.shape
    slots = 1 << BITS
    rows = TILE // slots
    half = slots // 2
    vox = lax.axis_index("vox")
    grams, rest = layout(batch, atoms)
    kinds = []
    for pairs, plain in grams + [rest]:
        kinds += [(pair, True) for pair in pairs] + [(tile, False) for tile in plain]
    split = len(kinds) - len(rest[0]) - len(rest[1])
    spare = jnp.zeros((SPARE, TILE), F32)
    for o in range(slots):
        source = mine_ref if o < half else other_ref
        start = (slot_of(vox ^ (o // half)) ^ (o % half)) * rows
        base = o % half * (len(kinds) * rows + SPARE)
        packed = 0
        for k, ((r, c), pair) in enumerate(kinds):
            at = base + k * rows + (SPARE if k >= split else 0)
            value = source[at:at + rows, :]
            if pair:
                stage[pl.ds(pl.multiple_of(packed * TILE + start, rows), rows), :] = value
                packed += 1
            else:
                full[pl.ds(pl.multiple_of(r * TILE + start, rows), rows), c * TILE:(c + 1) * TILE] = value
        spare = spare + source[base + split * rows:base + split * rows + SPARE, :]
    across, down = eye_tile()
    own = len(grams[0][0])
    mate = lax.axis_index("fold") & 1
    packed = 0
    for k, ((r, c), pair) in enumerate(kinds):
        if pair:
            value = stage[packed * TILE:(packed + 1) * TILE, :]
            turned = value.T
            if packed < 2 * own:
                at = packed // own * (SPARE // 2) + packed % own
                diagonal = spare[at:at + 1, :]
            else:
                at = own + packed - 2 * own
                diagonal = jnp.where(mate == 0, spare[at:at + 1, :], spare[at + SPARE // 2:at + SPARE // 2 + 1, :])
            packed += 1
            full[r * TILE:(r + 1) * TILE, r * TILE:(r + 1) * TILE] = jnp.where(across <= down, value, turned)
            full[c * TILE:(c + 1) * TILE, c * TILE:(c + 1) * TILE] = jnp.where(
                across == down, diagonal, jnp.where(across > down, value, turned))
        elif r * TILE >= batch or c * TILE < batch:
            full[c * TILE:(c + 1) * TILE, r * TILE:(r + 1) * TILE] = full[r * TILE:(r + 1) * TILE, c * TILE:(c + 1) * TILE].T

    gram = full[batch:, batch:]
    bound = top_row_sum(gram)
    inverse = 1.0 / bound
    limit = PENALTY * inverse
    g = halves(gram)
    corr = full[:batch, batch:]
    moved = corr * inverse
    code = moved - jnp.clip(moved, -limit, limit)
    groups = [slice(0, batch // 2), slice(batch // 2, batch)]
    codes = [code[group] for group in groups]
    for _ in range(ISTA_STEPS - 1):
        for j, group in enumerate(groups):
            moved = codes[j] - (dot3(halves(codes[j]), g) - corr[group]) * inverse
            codes[j] = moved - jnp.clip(moved, -limit, limit)
    code = jnp.concatenate(codes, axis=0)
    code_ref[...] = code
    code_copy = pltpu.make_async_copy(code_ref, code_hbm, sems.at[0])
    code_copy.start()

    x = halves(code)
    weighted = code * jnp.concatenate([weight_ref[...]] * (atoms // TILE), axis=1)
    w = halves(weighted)
    turned_w = halves(weighted.T)
    fit = corr - dot3(x, g)

    def residuals(corr_now, now):
        both = dot3(halves(jnp.concatenate([corr_now, now], axis=0)), x, NT)
        return full[:batch, :batch] - both[:batch], flipped_ref[...] - both[batch:]

    cross, rest = residuals(corr, dict_ref[...])
    step = 1.0 / (1.0 + top_row_sum(square3(turned_w, w)))
    square = cross - dot3(x, halves(fit), NT)
    tile_eye = across == down
    squares = jnp.concatenate(
        [jnp.sum(jnp.where(tile_eye, gram[r:r + TILE, r:r + TILE], 0.0), axis=0, keepdims=True)
         for r in range(0, atoms, TILE)], axis=1)
    moves = dot3(halves(jnp.concatenate([square, cross, rest], axis=0)), w)
    change = fit + (0.5 * step) * moves[:batch]
    squares = squares + 2.0 * step * jnp.sum(weighted * change, axis=0, keepdims=True)
    scale = 1.0 / jnp.sqrt(jnp.maximum(squares, 1.0))
    outer = dot3(turned_w, halves(change))
    corr = (corr + step * moves[batch:2 * batch]) * scale
    now = (dict_ref[...] + step * moves[2 * batch:]) * scale
    new_ref[...] = now
    cross, rest = residuals(corr, now)
    gram = (gram + step * (outer + outer.T)) * scale * column(scale)
    fit = corr - dot3(x, halves(gram))
    square = cross - dot3(x, halves(fit), NT)
    squares = squares * scale * scale
    moves = dot3(halves(jnp.concatenate([square, rest], axis=0)), w)
    change = fit + (0.5 * step) * moves[:batch]
    squares = squares + 2.0 * step * jnp.sum(weighted * change, axis=0, keepdims=True)
    scale = 1.0 / jnp.sqrt(jnp.maximum(squares, 1.0))
    copies = [code_copy]
    block = voxels // 3 if voxels % 3 == 0 and (voxels // 3) % 16 == 0 else voxels
    for j in range(voxels // block):
        here = slice(j * block, (j + 1) * block)
        new_ref[here, :] = (new_ref[here, :] + step * moves[batch + j * block:batch + (j + 1) * block]) * scale
        copies.append(pltpu.make_async_copy(new_ref.at[here, :], new_hbm.at[here, :], sems.at[2 + j]))
        copies[-1].start()
    outer = dot3(turned_w, halves(change))
    gram_ref[...] = (gram + step * (outer + outer.T)) * scale * column(scale)
    copies.append(pltpu.make_async_copy(gram_ref, gram_hbm, sems.at[1]))
    copies[-1].start()
    for copy in copies:
        copy.wait()


def all_reduce(keep, send, gram_rows, devices, folds):
    def swap(x, bit):
        bits = bit if isinstance(bit, tuple) else (bit, bit)
        return lax.ppermute(x, "vox", [(i, i ^ bits[i % 2]) for i in range(devices)])

    total = keep + swap(send, 1)
    slot = total.shape[0] // (len(SQUARE) + 1)
    own = total[:slot]
    got = [swap(total[(k + 1) * slot:(k + 2) * slot], bit) for k, bit in enumerate(SQUARE)]
    got = lax.optimization_barrier((got[2], got[0], got[1]))
    for part in got:
        own = own + part
    head = gram_rows + SPARE
    cut = head + 2 * SPARE
    gram, rest = lax.optimization_barrier((own[:cut], own[cut:]))
    for k in range(BITS, devices.bit_length() - 1):
        bit = 3 << (k - 1) if k == BITS else 1 << k
        other = swap(gram, bit), swap(rest, bit)
        gram, rest = gram + other[0], rest + other[1]
    next_gram = lax.ppermute(gram[:head], "fold", [(i, i ^ 1) for i in range(folds)])
    next_gram, rest = lax.optimization_barrier((next_gram, rest))
    even = lax.axis_index("fold") & 1 == 0
    first = jnp.where(even, gram[:gram_rows], next_gram[:gram_rows])
    second = jnp.where(even, next_gram[:gram_rows], gram[:gram_rows])
    own = jnp.concatenate([first, second, gram[gram_rows:head] + next_gram[gram_rows:], gram[head:], rest])
    ahead, across, along = (swap(own, bit) for bit in SQUARE)
    across, along, ahead = lax.optimization_barrier((across, along, ahead))
    mine = jnp.concatenate([own, ahead, across, along])
    return mine, swap(mine, 1)


def pin(x):
    return pltpu.with_memory_space_constraint(x, pltpu.HBM)


def shards(devices, folds, volumes, record_index, fold_of, held_out, dictionary):
    records, voxels = volumes.shape
    batch = record_index.shape[0]
    atoms = dictionary.shape[1]
    grams, rest = layout(batch, atoms)
    gram_tiles, rest_tiles = (len(pairs) + len(plain) for pairs, plain in (grams[0], rest))
    slots = 1 << BITS
    part = jax.ShapeDtypeStruct((slots // 2 * ((gram_tiles + rest_tiles) * TILE // slots + SPARE), TILE), F32)
    vmem = pl.BlockSpec(memory_space=pltpu.VMEM)
    smem = pl.BlockSpec(memory_space=pltpu.SMEM)
    hbm = pl.BlockSpec(memory_space=pltpu.HBM)
    params = pltpu.CompilerParams(vmem_limit_bytes=48 << 20)
    keep, send, flipped, weight = pl.pallas_call(
        gram_kernel,
        out_shape=(part, part, jax.ShapeDtypeStruct((voxels, batch), F32), jax.ShapeDtypeStruct((batch, TILE), F32)),
        in_specs=[hbm, hbm, smem, hbm, hbm],
        out_specs=(vmem,) * 4,
        scratch_shapes=[pltpu.VMEM((1, batch), jnp.int32), pltpu.VMEM((1, records), jnp.int32),
                        pltpu.VMEM(volumes.shape, F32), pltpu.VMEM(dictionary.shape, F32),
                        pltpu.VMEM(((gram_tiles + rest_tiles) * TILE, TILE), F32),
                        pltpu.SemaphoreType.DMA((4,))],
        compiler_params=params,
        name="grams",
    )(pin(record_index[None]), pin(fold_of[None]), held_out, pin(volumes), pin(dictionary))
    mine, other = all_reduce(keep, send, gram_tiles * TILE // slots, devices, folds)
    outs = [dictionary.shape, (batch, atoms), (atoms, atoms)]
    return pl.pallas_call(
        step_kernel,
        out_shape=tuple(jax.ShapeDtypeStruct(shape, F32) for shape in outs),
        in_specs=[vmem] * 5,
        out_specs=(hbm,) * 3,
        scratch_shapes=[pltpu.VMEM((batch + atoms, batch + atoms), F32), pltpu.VMEM(((batch + atoms) // 2, TILE), F32)]
        + [pltpu.VMEM(shape, F32) for shape in outs] + [pltpu.SemaphoreType.DMA((5,))],
        compiler_params=params,
        name="step",
    )(mine, other, flipped, weight, dictionary)


def solution(mesh):
    in_specs = (P("fold", "vox"), P("fold"), P("fold"), P("fold"), P("vox", None))
    out_specs = (P(("fold", "vox"), None), P("fold", None), P("fold", None))
    return jax.shard_map(functools.partial(shards, mesh.shape["vox"], mesh.shape["fold"]), mesh=mesh, in_specs=in_specs, out_specs=out_specs, check_vma=False)
```

```python
import functools

import jax
import jax.numpy as jnp
from jax import lax
from jax.experimental import pallas as pl
from jax.experimental.pallas import tpu as pltpu
from jax.sharding import PartitionSpec as P

ISTA_STEPS = 5
PENALTY = 0.5
TILE = 128
SPARE = 8
BITS = 3
SQUARE = ((4, 2), (6, 6), (2, 4))
F32 = jnp.float32
BF16 = jnp.bfloat16

NN = (((1,), (0,)), ((), ()))
TN = (((0,), (0,)), ((), ()))
NT = (((1,), (1,)), ((), ()))


def halves(x):
    hi = x.astype(BF16)
    return hi, (x - hi.astype(F32)).astype(BF16)


def dot1(a, b, dims=NN):
    return lax.dot_general(a, b, dims, preferred_element_type=F32)


def dot3(a, b, dims=NN):
    (left,), _ = dims[0]
    rows = a[0].shape[1 - left]
    both = dot1(jnp.concatenate(a, axis=1 - left), b[0], dims)
    return both[:rows] + (both[rows:] + dot1(a[0], b[1], dims))


def square3(a, b, dims=NN):
    mixed = dot1(a[0], b[1], dims)
    return dot1(a[0], b[0], dims) + (mixed + mixed.T)


def top_row_sum(x):
    return jnp.max(jnp.sum(jnp.abs(x), axis=0, keepdims=True), axis=1, keepdims=True)


def upper_tiles(first, count):
    ends = range(first, first + count)
    return [(r, c) for r in ends for c in ends if c > r], [(r, r + 1) for r in ends[::2]]


def layout(batch, atoms):
    edge, wide = batch // TILE, atoms // TILE
    grams = []
    for fold in range(2):
        plain, pairs = upper_tiles(edge + fold * wide // 2, wide // 2)
        strip = range(edge + fold * wide // 4, edge + (fold + 1) * wide // 4)
        plain = plain + [(r, c) for r in strip for c in range(edge + wide // 2, edge + wide)]
        grams.append((pairs, plain))
    plain, pairs = upper_tiles(0, edge)
    rest = (pairs, plain + [(r, c) for r in range(edge) for c in range(edge, edge + wide)])
    return grams, rest


def slot_of(vox):
    core = vox & 1
    x = (vox >> 1) & 1
    z = ((vox >> 2) ^ (vox >> 3)) & 1
    return core * 4 + (x + core * (z - x)) * 2 + (x ^ z)


def column(row):
    return jnp.broadcast_to(row, (TILE, row.shape[1])).T[:, :1]


def eye_tile():
    rows = lax.broadcasted_iota(jnp.int32, (TILE, TILE), 0)
    columns = lax.broadcasted_iota(jnp.int32, (TILE, TILE), 1)
    return rows, columns


def pack(pairs, plain, block, first, stage, at):
    rows, columns = eye_tile()

    def tile(r, c):
        r, c = (r - first[0]) * TILE, (c - first[1]) * TILE
        return block[r:r + TILE, c:c + TILE]

    apart = []
    for one, other in pairs:
        low = tile(other, other)
        stage[at * TILE:(at + 1) * TILE, :] = jnp.where(rows <= columns, tile(one, one), low)
        apart.append(jnp.sum(jnp.where(rows == columns, low, 0.0), axis=0, keepdims=True))
        at += 1
    for r, c in plain:
        stage[at * TILE:(at + 1) * TILE, :] = tile(r, c)
        at += 1
    return apart, at


def gram_kernel(index_hbm, fold_hbm, held_ref, volumes_hbm, dict_hbm,
                keep_ref, send_ref, flipped_ref, weight_ref, index_ref, fold_ref, volumes_ref, dict_ref, stage, sems):
    pairs = ((index_hbm, index_ref), (fold_hbm, fold_ref), (volumes_hbm, volumes_ref), (dict_hbm, dict_ref))
    copies = [pltpu.make_async_copy(source, target, sems.at[j]) for j, (source, target) in enumerate(pairs)]
    for copy in copies:
        copy.start()
    batch = index_ref.shape[1]
    records = volumes_ref.shape[0]
    atoms = dict_ref.shape[1]
    edge = batch // TILE
    wide = atoms // TILE
    grams, (rest_pairs, rest_plain) = layout(batch, atoms)
    fold = lax.axis_index("fold") & 1
    for copy in copies[:-1]:
        copy.wait()
    pick = lax.broadcasted_iota(jnp.int32, (records, batch), 0) == index_ref[...]
    pick = pick.astype(F32).astype(BF16)
    v = halves(volumes_ref[...])
    b = (dot1(pick, v[0], TN), dot1(pick, v[1], TN))
    flipped_ref[...] = (b[0] + b[1]).T
    b = (b[0].astype(BF16), b[1].astype(BF16))
    copies[-1].wait()
    d = halves(dict_ref[...])
    far = slice(atoms // 2, atoms)
    mine = halves(dict_ref[:, pl.ds(pl.multiple_of(fold * (atoms // 2), TILE), atoms // 2)])
    strip = halves(dict_ref[:, pl.ds(pl.multiple_of(fold * (atoms // 4), TILE), atoms // 4)])
    near, plain = grams[0]
    apart, at = pack(near, [t for t in plain if t[1] < edge + wide // 2], square3(mine, mine, TN), (edge, edge), stage, 0)
    _, at = pack([], [t for t in plain if t[1] >= edge + wide // 2],
                 dot3(strip, (d[0][:, far], d[1][:, far]), TN), (edge, edge + wide // 2), stage, at)
    first = at
    own, at = pack(rest_pairs, [t for t in rest_plain if t[1] < edge], square3(b, b, NT), (0, 0), stage, at)
    _, at = pack([], [t for t in rest_plain if t[1] >= edge], dot3(b, d), (0, edge), stage, at)
    folds = jnp.broadcast_to(fold_ref[...], (TILE, records)).astype(F32).astype(BF16)
    folds = dot1(pick, folds, (((0,), (1,)), ((), ())))
    weight_ref[...] = jnp.where(folds != held_ref[0].astype(F32), 1.0, 0.0)

    place = lax.broadcasted_iota(jnp.int32, (SPARE, TILE), 0) - fold * (SPARE // 2)
    spare = jnp.zeros((SPARE, TILE), F32)
    for j, row in enumerate(apart + own):
        spare = spare + jnp.where(place == j, row, 0.0)
    slots = 1 << BITS
    rows = TILE // slots
    vox = lax.axis_index("vox")
    half = slots // 2
    for o in range(slots):
        out = keep_ref if o < half else send_ref
        which = slot_of(vox ^ (o // half)) ^ (o % half)
        base = o % half * (at * rows + SPARE)
        for k in range(at):
            to = base + k * rows + (SPARE if k >= first else 0)
            out[to:to + rows, :] = stage[pl.ds(pl.multiple_of(k * TILE + which * rows, rows), rows), :]
        out[base + first * rows:base + first * rows + SPARE, :] = jnp.where(which == 0, spare, 0.0)


def step_kernel(mine_ref, other_ref, flipped_ref, weight_ref, dict_ref,
                new_hbm, code_hbm, gram_hbm, full, stage, new_ref, code_ref, gram_ref, sems):
    batch = flipped_ref.shape[1]
    voxels, atoms = dict_ref.shape
    slots = 1 << BITS
    rows = TILE // slots
    half = slots // 2
    vox = lax.axis_index("vox")
    grams, rest = layout(batch, atoms)
    kinds = []
    for pairs, plain in grams + [rest]:
        kinds += [(pair, True) for pair in pairs] + [(tile, False) for tile in plain]
    split = len(kinds) - len(rest[0]) - len(rest[1])
    spare = jnp.zeros((SPARE, TILE), F32)
    for o in range(slots):
        source = mine_ref if o < half else other_ref
        start = (slot_of(vox ^ (o // half)) ^ (o % half)) * rows
        base = o % half * (len(kinds) * rows + SPARE)
        packed = 0
        for k, ((r, c), pair) in enumerate(kinds):
            at = base + k * rows + (SPARE if k >= split else 0)
            value = source[at:at + rows, :]
            if pair:
                stage[pl.ds(pl.multiple_of(packed * TILE + start, rows), rows), :] = value
                packed += 1
            else:
                full[pl.ds(pl.multiple_of(r * TILE + start, rows), rows), c * TILE:(c + 1) * TILE] = value
        spare = spare + source[base + split * rows:base + split * rows + SPARE, :]
    across, down = eye_tile()
    own = len(grams[0][0])
    mate = lax.axis_index("fold") & 1
    packed = 0
    for k, ((r, c), pair) in enumerate(kinds):
        if pair:
            value = stage[packed * TILE:(packed + 1) * TILE, :]
            turned = value.T
            if packed < 2 * own:
                at = packed // own * (SPARE // 2) + packed % own
                diagonal = spare[at:at + 1, :]
            else:
                at = own + packed - 2 * own
                diagonal = jnp.where(mate == 0, spare[at:at + 1, :], spare[at + SPARE // 2:at + SPARE // 2 + 1, :])
            packed += 1
            full[r * TILE:(r + 1) * TILE, r * TILE:(r + 1) * TILE] = jnp.where(across <= down, value, turned)
            full[c * TILE:(c + 1) * TILE, c * TILE:(c + 1) * TILE] = jnp.where(
                across == down, diagonal, jnp.where(across > down, value, turned))
        elif r * TILE >= batch or c * TILE < batch:
            full[c * TILE:(c + 1) * TILE, r * TILE:(r + 1) * TILE] = full[r * TILE:(r + 1) * TILE, c * TILE:(c + 1) * TILE].T

    gram = full[batch:, batch:]
    bound = top_row_sum(gram)
    inverse = 1.0 / bound
    limit = PENALTY * inverse
    g = halves(gram)
    corr = full[:batch, batch:]
    moved = corr * inverse
    code = moved - jnp.clip(moved, -limit, limit)
    groups = [slice(0, batch // 2), slice(batch // 2, batch)]
    codes = [code[group] for group in groups]
    for _ in range(ISTA_STEPS - 1):
        for j, group in enumerate(groups):
            moved = codes[j] - (dot3(halves(codes[j]), g) - corr[group]) * inverse
            codes[j] = moved - jnp.clip(moved, -limit, limit)
    code = jnp.concatenate(codes, axis=0)
    code_ref[...] = code
    code_copy = pltpu.make_async_copy(code_ref, code_hbm, sems.at[0])
    code_copy.start()

    x = halves(code)
    weighted = code * jnp.concatenate([weight_ref[...]] * (atoms // TILE), axis=1)
    w = halves(weighted)
    turned_w = halves(weighted.T)
    fit = corr - dot3(x, g)

    def residuals(corr_now, now):
        both = dot3(halves(jnp.concatenate([corr_now, now], axis=0)), x, NT)
        return full[:batch, :batch] - both[:batch], flipped_ref[...] - both[batch:]

    cross, rest = residuals(corr, dict_ref[...])
    step = 1.0 / (1.0 + top_row_sum(square3(turned_w, w)))
    square = cross - dot3(x, halves(fit), NT)
    tile_eye = across == down
    squares = jnp.concatenate(
        [jnp.sum(jnp.where(tile_eye, gram[r:r + TILE, r:r + TILE], 0.0), axis=0, keepdims=True)
         for r in range(0, atoms, TILE)], axis=1)
    moves = dot3(halves(jnp.concatenate([square, cross, rest], axis=0)), w)
    change = fit + (0.5 * step) * moves[:batch]
    squares = squares + 2.0 * step * jnp.sum(weighted * change, axis=0, keepdims=True)
    scale = 1.0 / jnp.sqrt(jnp.maximum(squares, 1.0))
    outer = dot3(turned_w, halves(change))
    corr = (corr + step * moves[batch:2 * batch]) * scale
    now = (dict_ref[...] + step * moves[2 * batch:]) * scale
    new_ref[...] = now
    cross, rest = residuals(corr, now)
    gram = (gram + step * (outer + outer.T)) * scale * column(scale)
    fit = corr - dot3(x, halves(gram))
    square = cross - dot3(x, halves(fit), NT)
    squares = squares * scale * scale
    moves = dot3(halves(jnp.concatenate([square, rest], axis=0)), w)
    change = fit + (0.5 * step) * moves[:batch]
    squares = squares + 2.0 * step * jnp.sum(weighted * change, axis=0, keepdims=True)
    scale = 1.0 / jnp.sqrt(jnp.maximum(squares, 1.0))
    copies = [code_copy]
    block = voxels // 3 if voxels % 3 == 0 and (voxels // 3) % 16 == 0 else voxels
    for j in range(voxels // block):
        here = slice(j * block, (j + 1) * block)
        new_ref[here, :] = (new_ref[here, :] + step * moves[batch + j * block:batch + (j + 1) * block]) * scale
        copies.append(pltpu.make_async_copy(new_ref.at[here, :], new_hbm.at[here, :], sems.at[2 + j]))
        copies[-1].start()
    outer = dot3(turned_w, halves(change))
    gram_ref[...] = (gram + step * (outer + outer.T)) * scale * column(scale)
    copies.append(pltpu.make_async_copy(gram_ref, gram_hbm, sems.at[1]))
    copies[-1].start()
    for copy in copies:
        copy.wait()


def all_reduce(keep, send, gram_rows, devices, folds):
    def swap(x, bit):
        bits = bit if isinstance(bit, tuple) else (bit, bit)
        return lax.ppermute(x, "vox", [(i, i ^ bits[i % 2]) for i in range(devices)])

    total = keep + swap(send, 1)
    slot = total.shape[0] // (len(SQUARE) + 1)
    own = total[:slot]
    got = [swap(total[(k + 1) * slot:(k + 2) * slot], bit) for k, bit in enumerate(SQUARE)]
    got = lax.optimization_barrier((got[2], got[0], got[1]))
    for part in got:
        own = own + part
    head = gram_rows + SPARE
    cut = head + SPARE
    gram, rest = lax.optimization_barrier((own[:cut], own[cut:]))
    for k in range(BITS, devices.bit_length() - 1):
        bit = 3 << (k - 1) if k == BITS else 1 << k
        other = swap(gram, bit), swap(rest, bit)
        gram, rest = gram + other[0], rest + other[1]
    next_gram = lax.ppermute(gram[:head], "fold", [(i, i ^ 1) for i in range(folds)])
    next_gram, rest = lax.optimization_barrier((next_gram, rest))
    even = lax.axis_index("fold") & 1 == 0
    first = jnp.where(even, gram[:gram_rows], next_gram[:gram_rows])
    second = jnp.where(even, next_gram[:gram_rows], gram[:gram_rows])
    own = jnp.concatenate([first, second, gram[gram_rows:head] + next_gram[gram_rows:], gram[head:], rest])
    ahead, across, along = (swap(own, bit) for bit in SQUARE)
    along, ahead, across = lax.optimization_barrier((along, ahead, across))
    mine = jnp.concatenate([own, ahead, across, along])
    return mine, swap(mine, 1)


def pin(x):
    return pltpu.with_memory_space_constraint(x, pltpu.HBM)


def shards(devices, folds, volumes, record_index, fold_of, held_out, dictionary):
    records, voxels = volumes.shape
    batch = record_index.shape[0]
    atoms = dictionary.shape[1]
    grams, rest = layout(batch, atoms)
    gram_tiles, rest_tiles = (len(pairs) + len(plain) for pairs, plain in (grams[0], rest))
    slots = 1 << BITS
    part = jax.ShapeDtypeStruct((slots // 2 * ((gram_tiles + rest_tiles) * TILE // slots + SPARE), TILE), F32)
    vmem = pl.BlockSpec(memory_space=pltpu.VMEM)
    smem = pl.BlockSpec(memory_space=pltpu.SMEM)
    hbm = pl.BlockSpec(memory_space=pltpu.HBM)
    params = pltpu.CompilerParams(vmem_limit_bytes=48 << 20)
    keep, send, flipped, weight = pl.pallas_call(
        gram_kernel,
        out_shape=(part, part, jax.ShapeDtypeStruct((voxels, batch), F32), jax.ShapeDtypeStruct((batch, TILE), F32)),
        in_specs=[hbm, hbm, smem, hbm, hbm],
        out_specs=(vmem,) * 4,
        scratch_shapes=[pltpu.VMEM((1, batch), jnp.int32), pltpu.VMEM((1, records), jnp.int32),
                        pltpu.VMEM(volumes.shape, F32), pltpu.VMEM(dictionary.shape, F32),
                        pltpu.VMEM(((gram_tiles + rest_tiles) * TILE, TILE), F32),
                        pltpu.SemaphoreType.DMA((4,))],
        compiler_params=params,
        name="grams",
    )(pin(record_index[None]), pin(fold_of[None]), held_out, pin(volumes), pin(dictionary))
    mine, other = all_reduce(keep, send, gram_tiles * TILE // slots, devices, folds)
    outs = [dictionary.shape, (batch, atoms), (atoms, atoms)]
    return pl.pallas_call(
        step_kernel,
        out_shape=tuple(jax.ShapeDtypeStruct(shape, F32) for shape in outs),
        in_specs=[vmem] * 5,
        out_specs=(hbm,) * 3,
        scratch_shapes=[pltpu.VMEM((batch + atoms, batch + atoms), F32), pltpu.VMEM(((batch + atoms) // 2, TILE), F32)]
        + [pltpu.VMEM(shape, F32) for shape in outs] + [pltpu.SemaphoreType.DMA((5,))],
        compiler_params=params,
        name="step",
    )(mine, other, flipped, weight, dictionary)


def solution(mesh):
    in_specs = (P("fold", "vox"), P("fold"), P("fold"), P("fold"), P("vox", None))
    out_specs = (P(("fold", "vox"), None), P("fold", None), P("fold", None))
    return jax.shard_map(functools.partial(shards, mesh.shape["vox"], mesh.shape["fold"]), mesh=mesh, in_specs=in_specs, out_specs=out_specs, check_vma=False)
```
